32 devices in a mesh: group: 8 (over z, y), mp: 4 (over x, core).
Axes of the slice: x: 2, y: 2, z: 4, core: 2. Of those that a mesh axis runs over, the one named last changes fastest.
Arguments:
- tokens: bfloat16 [16, 1024, 1152], P('group', 'mp'), may hold values from -6 to 6
- cotangent: bfloat16 [16, 1024, 1152], P('group', 'mp'), may hold values from -6 to 6
- key_mask: int32 [16, 1024], P('group'), may hold values from 0 to 1, as said below
- group_bucket: int32 [8], P('group'), may hold values from 0 to 15
- group_count: int32 [8], P('group'), may hold values from 1 to 2, as said below
- time_table: float32 [16, 1152], replicated, may hold values from -6 to 6
- ln_params: float32 [2, 4, 1152], replicated, may hold values from -1.5 to 2.1, as said below
- ln_first: float32 [2, 4, 1152], replicated, may hold values from -96 to 96
- ln_second: float32 [2, 4, 1152], replicated, may hold values from 128 to 1024
- rel_table: float32 [2, 16, 2, 63], replicated, may hold values from -5 to 5
- rel_first: float32 [2, 16, 2, 63], replicated, may hold values from -20 to 20
- rel_second: float32 [2, 16, 2, 63], replicated, may hold values from 6.4 to 25.6
- qkv_weight: float32 [2, 1152, 3, 1152], P(None, 'group', None, 'mp')
- qkv_first: float32 [2, 1152, 3, 1152], P(None, 'group', None, 'mp'), may hold values from -96 to 96
- qkv_second: float32 [2, 1152, 3, 1152], P(None, 'group', None, 'mp'), may hold values from 128 to 1024
- time_weight: float32 [2, 1152, 2, 1152], P(None, 'group', None, 'mp')
- time_first: float32 [2, 1152, 2, 1152], P(None, 'group', None, 'mp'), may hold values from -96 to 96
- time_second: float32 [2, 1152, 2, 1152], P(None, 'group', None, 'mp'), may hold values from 128 to 1024
- out_weight: float32 [2, 1152, 1152], P(None, 'mp', 'group')
- out_first: float32 [2, 1152, 1152], P(None, 'mp', 'group'), may hold values from -96 to 96
- out_second: float32 [2, 1152, 1152], P(None, 'mp', 'group'), may hold values from 128 to 1024
- up_weight: float32 [2, 1152, 4608], P(None, 'group', 'mp')
- up_first: float32 [2, 1152, 4608], P(None, 'group', 'mp'), may hold values from -96 to 96
- up_second: float32 [2, 1152, 4608], P(None, 'group', 'mp'), may hold values from 128 to 1024
- down_weight: float32 [2, 4608, 1152], P(None, 'mp', 'group')
- down_first: float32 [2, 4608, 1152], P(None, 'mp', 'group'), may hold values from -96 to 96
- down_second: float32 [2, 4608, 1152], P(None, 'mp', 'group'), may hold values from 128 to 1024
Outputs:
- block_out: bfloat16 [16, 1024, 1152], P('group', 'mp')
- tokens_grad: bfloat16 [16, 1024, 1152], P('group', 'mp')
- ln_new: float32 [2, 4, 1152], replicated
- ln_first_new: float32 [2, 4, 1152], replicated
- ln_second_new: float32 [2, 4, 1152], replicated
- rel_new: float32 [2, 16, 2, 63], replicated
- rel_first_new: float32 [2, 16, 2, 63], replicated
- rel_second_new: float32 [2, 16, 2, 63], replicated
- qkv_new: float32 [2, 1152, 3, 1152], P(None, 'group', None, 'mp')
- qkv_first_new: float32 [2, 1152, 3, 1152], P(None, 'group', None, 'mp')
- qkv_second_new: float32 [2, 1152, 3, 1152], P(None, 'group', None, 'mp')
- qkv_copy: bfloat16 [2, 1152, 3, 1152], P(None, 'group', None, 'mp')
- time_new: float32 [2, 1152, 2, 1152], P(None, 'group', None, 'mp')
- time_first_new: float32 [2, 1152, 2, 1152], P(None, 'group', None, 'mp')
- time_second_new: float32 [2, 1152, 2, 1152], P(None, 'group', None, 'mp')
- time_copy: bfloat16 [2, 1152, 2, 1152], P(None, 'group', None, 'mp')
- out_new: float32 [2, 1152, 1152], P(None, 'mp', 'group')
- out_first_new: float32 [2, 1152, 1152], P(None, 'mp', 'group')
- out_second_new: float32 [2, 1152, 1152], P(None, 'mp', 'group')
- out_copy: bfloat16 [2, 1152, 1152], P(None, 'mp', 'group')
- up_new: float32 [2, 1152, 4608], P(None, 'group', 'mp')
- up_first_new: float32 [2, 1152, 4608], P(None, 'group', 'mp')
- up_second_new: float32 [2, 1152, 4608], P(None, 'group', 'mp')
- up_copy: bfloat16 [2, 1152, 4608], P(None, 'group', 'mp')
- down_new: float32 [2, 4608, 1152], P(None, 'mp', 'group')
- down_first_new: float32 [2, 4608, 1152], P(None, 'mp', 'group')
- down_second_new: float32 [2, 4608, 1152], P(None, 'mp', 'group')
- down_copy: bfloat16 [2, 4608, 1152], P(None, 'mp', 'group')
- matrix_stats: float32 [3, 2, 5], replicated
The draws below stay inside these ranges and needn't reach their ends.
Inputs may be any that keep to these rules, and one draw needn't show every extreme that they name: Group g's live images are its first group_count[g] slots; in every draw some group has all 2 slots live and another only one. `key_mask`: an image's live keys are its first 256 positions or all 1024 of them; in every group some live image has all positions live. `ln_params`: rows 0 and 2 of each layer are positive gains, rows 1 and 3 are shifts.
All inputs are finite; a program needn't handle non-finite values.
Results may differ from the reference program's by a relative error of at most 0.02.
Values may be sent and summed in bfloat16 or wider, within the bound.
No kernel may reach another device: no remote copies, remote signals or barrier semaphores. Data moves between devices by JAX's collectives and lax.ppermute only.
A program may use at most 320 MiB of HBM per device.

```python
import math
import jax
import jax.numpy as jnp
from jax import lax

D = 1152
HEADS = 16
HEAD = 72
FF = 4608
SLOTS = 2
LAYERS = 2
BUCKETS = 16
STEP = 5
SEQ = 1024
REL = 63
GROUPS = 8
IMAGES = 16


def group_layout(key):
    groups = IMAGES // SLOTS
    key_one, key_two, key_three = jax.random.split(key, 3)
    counts = jax.random.randint(key_one, (groups,), 1, SLOTS + 1)
    busiest = jax.random.randint(key_two, (), 0, groups)
    lightest = (busiest + 1 + jax.random.randint(key_three, (), 0, groups - 1)) % groups
    places = jnp.arange(groups)
    counts = jnp.where(places == busiest, SLOTS, counts)
    counts = jnp.where(places == lightest, 1, counts)
    return counts.astype(jnp.int32)


def rising_profile(count, slope):
    ramp_up = jnp.arange(count, dtype=jnp.float32) / (count - 1)
    return (1.0 + slope * ramp_up) / (1.0 + slope + slope * slope / 3.0) ** 0.5


def ramped_matrix(key, shape, ramp_axis, fan_in, slope):
    values = jnp.clip(jax.random.normal(key, shape, jnp.float32), -4.0, 4.0) * fan_in ** (-0.5)
    profile_shape = [1] * len(shape)
    profile_shape[ramp_axis] = shape[ramp_axis]
    return values * rising_profile(shape[ramp_axis], slope).reshape(profile_shape)


def draw_group_count(key, part):
    return group_layout(key)


def draw_key_mask(key, part):
    counts = group_layout(key)
    key = jax.random.fold_in(key, 5)
    key_one, key_two = jax.random.split(key)
    groups = IMAGES // SLOTS
    chosen = jax.random.randint(key_one, (groups,), 0, SLOTS) % counts
    coin_flip = jax.random.randint(key_two, (groups, SLOTS), 0, 2)
    full_image = (coin_flip == 1) | (jnp.arange(SLOTS)[None, :] == chosen[:, None])
    length = jnp.where(full_image, SEQ, SEQ // 4).reshape(IMAGES)
    return (jnp.arange(SEQ)[None, :] < length[:, None]).astype(jnp.int32)


def draw_ln_params(key, part):
    key = jax.random.fold_in(key, 11)
    key_one, key_two = jax.random.split(key)
    slope = 2.0
    rising = rising_profile(D, slope)
    gain_rows = rising * jax.random.uniform(key_one, (LAYERS, 2, D), jnp.float32, 0.7, 1.3)
    shifts = 0.5 * jnp.clip(jax.random.normal(key_two, (LAYERS, 2, D), jnp.float32), -3.0, 3.0)
    return jnp.stack([gain_rows[:, 0], shifts[:, 0], gain_rows[:, 1], shifts[:, 1]], axis=1)


def draw_qkv_weight(key, part):
    key = jax.random.fold_in(key, 21)
    slope = 2.0
    return ramped_matrix(key, (LAYERS, D, 3, D), 1, D, slope)


def draw_time_weight(key, part):
    key = jax.random.fold_in(key, 22)
    slope = 2.0
    return ramped_matrix(key, (LAYERS, D, 2, D), 1, D, slope)


def draw_out_weight(key, part):
    key = jax.random.fold_in(key, 23)
    slope = 2.0
    return ramped_matrix(key, (LAYERS, D, D), 2, D, slope)


def draw_up_weight(key, part):
    key = jax.random.fold_in(key, 24)
    slope = 2.0
    return ramped_matrix(key, (LAYERS, D, FF), 1, D, slope)


def draw_down_weight(key, part):
    key = jax.random.fold_in(key, 25)
    slope = 2.0
    return ramped_matrix(key, (LAYERS, FF, D), 2, FF, slope)


def place_ends(drawn, key, smallest, top_value):
    longest = drawn.shape.index(max(drawn.shape))
    spots = []
    for shift in (0, 1):
        where = [jax.random.randint(jax.random.fold_in(key, axis), (), 0, length) for axis, length in enumerate(drawn.shape)]
        where[longest] = (where[longest] + shift) % drawn.shape[longest]
        spots.append(tuple(where))
    return drawn.at[spots[0]].set(smallest).at[spots[1]].set(top_value)


def level_of(own_key, dims, shards, low, largest):
    def one(position, blocks):
        draws = jax.random.uniform(jax.random.fold_in(jax.random.fold_in(own_key, 6), position), (blocks,), jnp.float32, low / len(shards), largest / len(shards))
        return jnp.repeat(jnp.exp(draws), dims[position] // blocks).reshape((-1,) + (1,) * (len(dims) - position - 1))

    gain = one(*shards[0])
    for cut in shards[1:]:
        gain = gain * one(*cut)
    return gain


def noise(own_key, dims, spread, limit, pieces=(), kind=jnp.bfloat16):
    loudness = level_of(own_key, dims, pieces, -0.22, 0.18) if pieces else 1.0
    entries = jax.random.normal(own_key, dims, jnp.float32) * spread * loudness
    return jnp.minimum(jnp.maximum(entries, -limit), limit).astype(kind)


def setup_inputs(seed: int = 0) -> dict:
    seeds = jax.random.split(jax.random.key(seed), 28)
    tokens = noise(seeds[0], (IMAGES, SEQ, D), 1.0, 6.0, ((0, 8), (1, 4)))
    cotangent = noise(seeds[1], (IMAGES, SEQ, D), 1.0, 6.0, ((0, 8), (1, 4)))
    key_mask = draw_key_mask(jax.random.fold_in(seeds[27], 71), 0)
    group_bucket = place_ends(jax.random.randint(seeds[3], (GROUPS,), 0, BUCKETS), jax.random.fold_in(seeds[3], 1), 0, BUCKETS - 1).astype(jnp.int32)
    group_count = draw_group_count(jax.random.fold_in(seeds[27], 71), 0)
    time_table = noise(seeds[5], (BUCKETS, D), 1.0, 6.0, (), jnp.float32)
    ln_params = draw_ln_params(jax.random.fold_in(seeds[27], 71), 0)
    ln_first = noise(seeds[7], (LAYERS, 4, D), (2 * (SEQ * IMAGES ** -1) ** 0.5), 96.0, (), jnp.float32)
    ln_second = jnp.clip(jnp.exp(jax.random.uniform(seeds[8], (LAYERS, 4, D), jnp.float32, math.log(128.0), math.log(1024.0))), 128.0, 1024.0)
    rel_table = noise(seeds[9], (LAYERS, HEADS, 2, REL), 0.7, 5.0, (), jnp.float32)
    rel_first = noise(seeds[10], (LAYERS, HEADS, 2, REL), (0.4 * (SEQ * IMAGES ** -1) ** 0.5), 20.0, (), jnp.float32)
    rel_second = jnp.clip(jnp.exp(jax.random.uniform(seeds[11], (LAYERS, HEADS, 2, REL), jnp.float32, math.log(6.4), math.log(25.6))), 6.4, 25.6)
    qkv_weight = draw_qkv_weight(jax.random.fold_in(seeds[27], 71), 0)
    qkv_first = noise(seeds[13], (LAYERS, D, 3, D), (2 * (SEQ * IMAGES ** -1) ** 0.5), 96.0, ((1, 8), (3, 4)), jnp.float32)
    qkv_second = jnp.clip(jnp.exp(math.log(1024.0) - 2.0794415 * jax.random.uniform(seeds[14], (LAYERS, D, 3, D), jnp.float32) ** level_of(seeds[14], (LAYERS, D, 3, D), ((1, 8), (3, 4)), -0.2, 0.2)), 128.0, 1024.0)
    time_weight = draw_time_weight(jax.random.fold_in(seeds[27], 71), 0)
    time_first = noise(seeds[16], (LAYERS, D, 2, D), (2 * (SEQ * IMAGES ** -1) ** 0.5), 96.0, ((1, 8), (3, 4)), jnp.float32)
    time_second = jnp.clip(jnp.exp(math.log(1024.0) - 2.0794415 * jax.random.uniform(seeds[17], (LAYERS, D, 2, D), jnp.float32) ** level_of(seeds[17], (LAYERS, D, 2, D), ((1, 8), (3, 4)), -0.2, 0.2)), 128.0, 1024.0)
    out_weight = draw_out_weight(jax.random.fold_in(seeds[27], 71), 0)
    out_first = noise(seeds[19], (LAYERS, D, D), (2 * (SEQ * IMAGES ** -1) ** 0.5), 96.0, ((1, 4), (2, 8)), jnp.float32)
    out_second = jnp.clip(jnp.exp(math.log(1024.0) - 2.0794415 * jax.random.uniform(seeds[20], (LAYERS, D, D), jnp.float32) ** level_of(seeds[20], (LAYERS, D, D), ((1, 4), (2, 8)), -0.2, 0.2)), 128.0, 1024.0)
    up_weight = draw_up_weight(jax.random.fold_in(seeds[27], 71), 0)
    up_first = noise(seeds[22], (LAYERS, D, FF), (2 * (SEQ * IMAGES ** -1) ** 0.5), 96.0, ((1, 8), (2, 4)), jnp.float32)
    up_second = jnp.clip(jnp.exp(math.log(1024.0) - 2.0794415 * jax.random.uniform(seeds[23], (LAYERS, D, FF), jnp.float32) ** level_of(seeds[23], (LAYERS, D, FF), ((1, 8), (2, 4)), -0.2, 0.2)), 128.0, 1024.0)
    down_weight = draw_down_weight(jax.random.fold_in(seeds[27], 71), 0)
    down_first = noise(seeds[25], (LAYERS, FF, D), (2 * (SEQ * IMAGES ** -1) ** 0.5), 96.0, ((1, 4), (2, 8)), jnp.float32)
    down_second = jnp.clip(jnp.exp(math.log(1024.0) - 2.0794415 * jax.random.uniform(seeds[26], (LAYERS, FF, D), jnp.float32) ** level_of(seeds[26], (LAYERS, FF, D), ((1, 4), (2, 8)), -0.2, 0.2)), 128.0, 1024.0)
    return dict(tokens=tokens, cotangent=cotangent, key_mask=key_mask, group_bucket=group_bucket, group_count=group_count, time_table=time_table, ln_params=ln_params, ln_first=ln_first, ln_second=ln_second, rel_table=rel_table, rel_first=rel_first, rel_second=rel_second, qkv_weight=qkv_weight, qkv_first=qkv_first, qkv_second=qkv_second, time_weight=time_weight, time_first=time_first, time_second=time_second, out_weight=out_weight, out_first=out_first, out_second=out_second, up_weight=up_weight, up_first=up_first, up_second=up_second, down_weight=down_weight, down_first=down_first, down_second=down_second)


highest = lax.Precision.HIGHEST
norm_epsilon = 1e-05
adam_epsilon = 1e-06
beta_first = 0.5
beta_second = 0.5
decay_rate = 0.01
learn_rate = 0.5

@jax.custom_vjp
def low(v):
    return lax.optimization_barrier(v.astype(jnp.bfloat16)).astype(jnp.float32)

@jax.custom_vjp
def low_back(v):
    return v

def low_keep(v):
    return (low(v), None)

def low_pass(kept, grad):
    return (grad,)

def back_keep(v):
    return (v, None)

def back_low(kept, grad):
    return (low(grad),)
low.defvjp(low_keep, low_pass)
low_back.defvjp(back_keep, back_low)

def norm_rows(inputs, norm_gain, norm_shift):
    average = lax.optimization_barrier(jnp.mean(inputs, axis=-1, keepdims=True))
    centred = inputs - average
    scaling = lax.rsqrt(lax.optimization_barrier(jnp.mean(centred * centred, axis=-1, keepdims=True)) + norm_epsilon)
    return centred * scaling * norm_gain + norm_shift

def offset_onehot(grid_side):
    places = jnp.arange(grid_side)
    offset = places[:, None] - places[None, :] + grid_side - 1
    return (offset[:, :, None] == jnp.arange(2 * grid_side - 1)[None, None, :]).astype(jnp.float32)

def relative_bias(rel_part):
    head_count = rel_part.shape[0]
    grid_side = (rel_part.shape[2] + 1) // 2
    onehot = offset_onehot(grid_side)
    row_bias = jnp.einsum('abr,hr->hab', onehot, rel_part[:, 0], precision=highest)
    col_bias = jnp.einsum('abr,hr->hab', onehot, rel_part[:, 1], precision=highest)
    whole = row_bias[:, :, None, :, None] + col_bias[:, None, :, None, :]
    return whole.reshape(head_count, grid_side * grid_side, grid_side * grid_side)

def attend(queries, keyset, values, live_keys, rel_bias):
    scaling = queries.shape[-1] ** (-0.5)
    scores = jnp.einsum('qhd,khd->hqk', queries, keyset, precision=highest) * scaling + rel_bias
    scores = low_back(scores)
    scores = jnp.where(live_keys[None, None, :] > 0, scores, -1e+30)
    row_max = lax.optimization_barrier(jnp.max(scores, axis=-1, keepdims=True))
    weights_exp = jnp.exp(scores - row_max)
    softmax_out = low(weights_exp / lax.optimization_barrier(jnp.sum(weights_exp, axis=-1, keepdims=True)))
    return jnp.einsum('hqk,khd->qhd', softmax_out, values, precision=highest)

def lamb_moments(param, first, second, gradient):
    first_new = beta_first * first + (1.0 - beta_first) * gradient
    second_new = beta_second * second + (1.0 - beta_second) * gradient * gradient
    corrected = first_new / (1.0 - beta_first ** STEP)
    update = corrected / (jnp.sqrt(second_new / (1.0 - beta_second ** STEP)) + adam_epsilon) + decay_rate * param
    return (first_new, second_new, update)

def reference(tokens, cotangent, key_mask, group_bucket, group_count, time_table, ln_params, ln_first, ln_second, rel_table, rel_first, rel_second, qkv_weight, qkv_first, qkv_second, time_weight, time_first, time_second, out_weight, out_first, out_second, up_weight, up_first, up_second, down_weight, down_first, down_second):
    groups = IMAGES // SLOTS
    bucket_hit = (group_bucket[:, None] == jnp.arange(BUCKETS)[None, :]).astype(jnp.float32)
    time_rows = low(jnp.dot(bucket_hit, time_table, precision=highest))
    image_time = jnp.repeat(time_rows, SLOTS, axis=0)
    slot_index = jnp.tile(jnp.arange(SLOTS), groups)
    live_slot = (slot_index < jnp.repeat(group_count, SLOTS)).astype(jnp.float32)
    start_grad = cotangent.astype(jnp.float32) * live_slot[:, None, None]
    params = (ln_params, rel_table, qkv_weight, time_weight, out_weight, up_weight, down_weight)

    def run(inputs, weights):
        norm_all, rel_all, qkv_all, time_all, out_all, up_all, down_all = weights
        state = inputs
        for layer_index in range(LAYERS):
            norm_params = norm_all[layer_index]
            first_norm = low(norm_rows(state, norm_params[0], norm_params[1]))
            time_shift = jnp.einsum('nd,dcf->ncf', image_time, low(time_all[layer_index]), precision=highest)
            project = jnp.einsum('snd,dcf->sncf', first_norm, low(qkv_all[layer_index]), precision=highest)
            queries = low_back(low(project[:, :, 0] + time_shift[:, None, 0])).reshape(IMAGES, SEQ, HEADS, HEAD)
            keyset = low_back(low(project[:, :, 1])).reshape(IMAGES, SEQ, HEADS, HEAD)
            values = low_back(low(project[:, :, 2] + time_shift[:, None, 1])).reshape(IMAGES, SEQ, HEADS, HEAD)
            rel_bias = relative_bias(rel_all[layer_index])
            attend_one = jax.checkpoint(lambda members: attend(members[0], members[1], members[2], members[3], rel_bias))
            mixed = lax.map(attend_one, (queries, keyset, values, key_mask)).reshape(IMAGES, SEQ, D)
            mixed = low_back(low(mixed))
            middle = state + low_back(jnp.einsum('snf,fd->snd', mixed, low(out_all[layer_index]), precision=highest))
            second_norm = low(norm_rows(middle, norm_params[2], norm_params[3]))
            pre_act = low_back(jnp.einsum('snd,df->snf', second_norm, low(up_all[layer_index]), precision=highest))
            active = low(jax.nn.gelu(pre_act, approximate=True))
            state = middle + low_back(jnp.einsum('snf,fd->snd', active, low(down_all[layer_index]), precision=highest))
        return state
    block_value, pullback = jax.vjp(run, tokens.astype(jnp.float32), params)
    input_grad, grads = pullback(start_grad)
    total = jnp.sum(group_count).astype(jnp.float32)
    inverse = 1.0 / total
    ln_grad = grads[0] * inverse
    ln_first_new, ln_second_new, ln_update = lamb_moments(ln_params, ln_first, ln_second, ln_grad)
    ln_ratio = jnp.sqrt(lax.optimization_barrier(jnp.sum(ln_params * ln_params, axis=-1, keepdims=True))) / jnp.sqrt(lax.optimization_barrier(jnp.sum(ln_update * ln_update, axis=-1, keepdims=True)))
    ln_new = ln_params - learn_rate * ln_ratio * ln_update
    rel_grad = grads[1] * inverse
    rel_first_new, rel_second_new, rel_update = lamb_moments(rel_table, rel_first, rel_second, rel_grad)
    rel_ratio = jnp.sqrt(lax.optimization_barrier(jnp.sum(rel_table * rel_table, axis=(1, 2, 3), keepdims=True))) / jnp.sqrt(lax.optimization_barrier(jnp.sum(rel_update * rel_update, axis=(1, 2, 3), keepdims=True)))
    rel_new = rel_table - learn_rate * rel_ratio * rel_update
    masters = (qkv_weight, time_weight, out_weight, up_weight, down_weight)
    first_olds = (qkv_first, time_first, out_first, up_first, down_first)
    second_olds = (qkv_second, time_second, out_second, up_second, down_second)
    results = []
    weight_norms = []
    update_norms = []
    ratios = []
    for matrix_index in range(5):
        master = masters[matrix_index]
        gradient = grads[2 + matrix_index] * inverse
        first_new, second_new, update = lamb_moments(master, first_olds[matrix_index], second_olds[matrix_index], gradient)
        summed_axes = tuple(range(1, master.ndim))
        weight_norm = jnp.sqrt(lax.optimization_barrier(jnp.sum(master * master, axis=summed_axes)))
        update_norm = jnp.sqrt(lax.optimization_barrier(jnp.sum(update * update, axis=summed_axes)))
        trust_ratio = weight_norm / update_norm
        factor = (learn_rate * trust_ratio).reshape((LAYERS,) + (1,) * (master.ndim - 1))
        renewed = master - factor * update
        results.extend([renewed, first_new, second_new, renewed.astype(jnp.bfloat16)])
        weight_norms.append(weight_norm)
        update_norms.append(update_norm)
        ratios.append(trust_ratio)
    matrix_stats = jnp.stack([jnp.stack(weight_norms, axis=1), jnp.stack(update_norms, axis=1), jnp.stack(ratios, axis=1)])
    return (block_value.astype(jnp.bfloat16), (input_grad * inverse).astype(jnp.bfloat16), ln_new, ln_first_new, ln_second_new, rel_new, rel_first_new, rel_second_new, results[0], results[1], results[2], results[3], results[4], results[5], results[6], results[7], results[8], results[9], results[10], results[11], results[12], results[13], results[14], results[15], results[16], results[17], results[18], results[19], matrix_stats)
```

```python
import functools

import jax
import jax.numpy as jnp
from jax import lax
from jax.experimental import pallas as pl
from jax.experimental.pallas import tpu as pltpu
from jax.sharding import PartitionSpec as P

STEP = 5
highest = lax.Precision.HIGHEST
norm_epsilon = 1e-05
adam_epsilon = 1e-06
beta_first = 0.5
beta_second = 0.5
decay_rate = 0.01
learn_rate = 0.5

HEAD = 72
SPARE = 256 - 3 * HEAD
LANE = 128
CHUNKS = 4
MIB = 1 << 20
MASKED = -1e30
SMALL = 6e7
BIG = 6e6
LOG2E = 1.4426950408889634
GELU_A = 0.7978845608
GELU_B = 0.044715
SCALE = HEAD**-0.5
ROOT = HEAD**0.5
EXP_SCALE = LOG2E * SCALE
SEQUENCE = (
    "i0", "i1", "unpack0", "i0", "i0", "i1", "i0", "p1",
    "i0", "i0", "i1", "p0", "i1", "i1", "i0", "unpack1",
    "p1", "i0", "i0", "i1", "p0", "i1", "i1", "i0",
    "p1", "i0", "i0", "i0", "i1", "i0", "i1", "i1",
    "i1", "up1", "i0", "i1", "i0", "down1", "i0", "i1",
    "p0", "i1", "i1", "out1", "i0", "p1", "i0", "qkv1",
    "i0", "i1", "p0", "i1", "i1", "hold_mlp1", "up0", "i0",
    "p1", "i0", "down0", "i0", "i1", "p0", "i1", "out0",
    "hold_attend1", "i1", "qkv0", "last", "i0", "i1", "i0", "i1",
    "i1", "e0", "e1",
)
bf16 = jnp.bfloat16
f32 = jnp.float32


def dot_nn(left, right):
    return lax.dot_general(left, right, (((1,), (0,)), ((), ())), preferred_element_type=f32)


def dot_nt(left, right):
    return lax.dot_general(left, right, (((1,), (1,)), ((), ())), preferred_element_type=f32)


def split_three(value):
    top = value.astype(bf16)
    rest = value - top.astype(f32)
    middle = rest.astype(bf16)
    last = (rest - middle.astype(f32)).astype(bf16)
    return top, middle, last


def lanes_of(shape):
    return lax.broadcasted_iota(jnp.int32, shape, len(shape) - 1)


def columns_spec(rows, columns, start):
    return pl.BlockSpec((pl.Element(rows), pl.Element(columns)), lambda step: (0, start))


def whole_spec(shape):
    return pl.BlockSpec(shape, lambda step: (0,) * len(shape))


class Chain:
    def __init__(self):
        self.token = None
        self.holds = []
        self.pending = None
        self.postpone = False

    def take_pair(self):
        return () if self.pending is None else self.pending.pop()

    def give_pair(self, result):
        if result:
            self.pending.append(result[0])
            self.pending = None

    def hold(self, *arrays):
        self.holds.extend(arrays)

    def call(self, body, grid, inputs, in_specs, out_specs, out_shape, scratch, flops, moved, exps, limit, name, aliases=None):
        count_in, count_out = len(in_specs), len(out_specs)
        waits = self.holds + ([] if self.token is None else [self.token])
        self.holds = []
        first = len(waits)

        def wrapped(*refs):
            ins = refs[first : first + count_in]
            outs = refs[first + count_in : first + count_in + count_out]
            token_ref = refs[first + count_in + count_out]
            rest = refs[first + count_in + count_out + 1 :]

            @pl.when(pl.program_id(0) == 0)
            def _():
                token_ref[...] = jnp.zeros(token_ref.shape, f32)

            body(*ins, *outs, *rest)

        token_spec = pl.BlockSpec((8, LANE), lambda *steps: (0, 0))
        results = pl.pallas_call(
            wrapped,
            grid=grid,
            in_specs=[pl.BlockSpec(memory_space=pl.ANY)] * first + in_specs,
            out_specs=out_specs + [token_spec],
            out_shape=out_shape + [jax.ShapeDtypeStruct((8, LANE), f32)],
            scratch_shapes=scratch,
            input_output_aliases={first + given: out for given, out in (aliases or {}).items()},
            compiler_params=pltpu.CompilerParams(vmem_limit_bytes=limit * MIB),
            cost_estimate=pl.CostEstimate(
                flops=int(flops), bytes_accessed=int(moved), transcendentals=int(exps)
            ),
            name=name,
        )(*waits, *inputs)
        self.token = results[-1]
        return results[:-1]


def put_half(half, value, keep_ref, send_ref):
    rows = keep_ref.shape[1]
    keep_ref[half] = value[:rows].astype(bf16)
    send_ref[half] = value[rows:].astype(bf16)


def row_half(own_ref, near_ref, half):
    return jnp.concatenate([own_ref[half], near_ref[half]], axis=0)


def unpack_body(packed_ref, out_ref):
    rows = packed_ref.shape[0]
    heads = out_ref.shape[1] // LANE
    lane = lanes_of((rows, LANE))
    rest = packed_ref[:, heads * 256 :].astype(f32)
    for head in range(heads):
        block = packed_ref[:, head * 256 : (head + 1) * 256].astype(f32)
        first = pltpu.roll(block, SPARE, 1)[:, :LANE]
        second = pltpu.roll(rest, (SPARE - head * (HEAD - SPARE)) % LANE, 1)
        value = jnp.where(lane < SPARE, first, jnp.where(lane < HEAD, second, 0.0))
        out_ref[:, head * LANE : (head + 1) * LANE] = value.astype(bf16)


def unpack_call(chain, packed, start, heads):
    width = packed.shape[0]
    rows = 384 if width % 384 == 0 else width
    columns = heads * (256 + HEAD - SPARE)
    return chain.call(
        unpack_body,
        (width // rows,),
        (packed,),
        [pl.BlockSpec((pl.Element(rows), pl.Element(columns)), lambda step: (step * rows, start))],
        [pl.BlockSpec((rows, heads * LANE), lambda step: (step, 0))],
        [jax.ShapeDtypeStruct((width, heads * LANE), bf16)],
        [],
        SMALL,
        1e3,
        0,
        63,
        "unpack_out",
    )[0]


def attend_body(
    own_ref, near_ref, w_ref, shift_ref, aux_ref, qpos_ref, kpos_ref, wo_ref,
    qkv_ref, mix_ref, keep_ref, send_ref,
):
    head = pl.program_id(0)
    heads = pl.num_programs(0)
    rows = own_ref.shape[1]
    seq = rows * CHUNKS
    weight = w_ref[...]

    block_rows = 2 * rows
    for half in range(2):
        where = pl.ds(half * block_rows, block_rows)
        out = dot_nn(row_half(own_ref, near_ref, half), weight) + shift_ref[0]
        lane = lanes_of((block_rows, LANE))
        keys = pltpu.roll(out, 256 - HEAD, 1)[:, :LANE]
        vals = pltpu.roll(out, 256 - 2 * HEAD, 1)[:, :LANE]
        queries = jnp.where(lane < HEAD, out[:, :LANE], jnp.where(lane == HEAD + 3, 1.0, 0.0))
        keys = jnp.where(lane < HEAD, keys, aux_ref[where, :].astype(f32))
        vals = jnp.where(lane < HEAD, vals, jnp.where(lane < HEAD + 3, 1.0, 0.0))
        qkv_ref[0, 0, where, :] = queries.astype(bf16)
        qkv_ref[0, 1, where, :] = keys.astype(bf16)
        qkv_ref[0, 2, where, :] = vals.astype(bf16)

    keyset = jnp.concatenate([qkv_ref[0, 1], kpos_ref[0]], axis=1)
    values = qkv_ref[0, 2]
    mix_lanes = pl.ds(pl.multiple_of(head * LANE, LANE), LANE)

    for start in range(0, seq, rows):
        where = pl.ds(start, rows)
        main = qkv_ref[0, 0, where, :]
        queries = jnp.concatenate([main, qpos_ref[where, :]], axis=1)
        scores = dot_nt(queries, keyset)
        top = jnp.max(scores, axis=1, keepdims=True)
        probs = jnp.exp2((scores - top) * EXP_SCALE).astype(bf16)
        mixed = dot_nn(probs, values)
        total = mixed[:, HEAD : HEAD + 1]
        lane = lanes_of((rows, LANE))
        mix_ref[where, mix_lanes] = jnp.where(lane < HEAD, mixed / total, 0.0).astype(bf16)
        hi, mid, low = split_three(-(top + jnp.log2(total) * (1.0 / EXP_SCALE)))
        main = jnp.where(lane == HEAD, hi, main)
        main = jnp.where(lane == HEAD + 1, mid, main)
        main = jnp.where(lane == HEAD + 2, low, main)
        qkv_ref[0, 0, where, :] = main

    @pl.when(head == heads - 1)
    def _():
        for half in range(2):
            where = pl.ds(half * block_rows, block_rows)
            put_half(half, dot_nt(mix_ref[where, :], wo_ref[...]), keep_ref, send_ref)


def attend_call(chain, pieces, weights, shift, aux, qpos, kpos):
    w_qkv, qkv_start = weights["attend"]
    w_out = weights["out"]
    _, rows, width = pieces[0].shape
    seq = rows * CHUNKS
    heads = kpos.shape[0]
    half = jax.ShapeDtypeStruct((2, rows, width), bf16)
    return chain.call(
        attend_body,
        (heads,),
        (*pieces, w_qkv, shift, aux, qpos, kpos, w_out),
        [whole_spec((2, rows, width))] * 2
        + [
            pl.BlockSpec((width, 256), lambda step: (0, qkv_start // 256 + step)),
            pl.BlockSpec((1, 1, 256), lambda step: (step, 0, 0)),
            whole_spec((seq, LANE)),
            whole_spec((seq, LANE)),
            pl.BlockSpec((1, seq, LANE), lambda step: (step, 0, 0)),
            whole_spec((width, heads * LANE)),
        ],
        [
            pl.BlockSpec((1, 3, seq, LANE), lambda step: (step, 0, 0, 0)),
            whole_spec((seq, heads * LANE)),
            whole_spec((2, rows, width)),
            whole_spec((2, rows, width)),
        ],
        [
            jax.ShapeDtypeStruct((heads, 3, seq, LANE), bf16),
            jax.ShapeDtypeStruct((seq, heads * LANE), bf16),
            half,
            half,
        ],
        [],
        BIG,
        1e3,
        0,
        63,
        "attend_fwd",
    )


def attend_back_body(
    own_ref, near_ref, wo_ref, qkv_ref, qpos_ref, kpos_ref, mix_ref, w_ref,
    dqkv_ref, sums_ref, rel_ref, keep_ref, send_ref,
    dmix, grad_vals, grad_keys, grad_queries,
):
    head = pl.program_id(0)
    heads = pl.num_programs(0)
    rows = own_ref.shape[1]
    seq = rows * CHUNKS
    grid_side = 32

    @pl.when(head == 0)
    def _():
        for half in range(2):
            where = pl.ds(half * 2 * rows, 2 * rows)
            dmix[where, :] = dot_nn(row_half(own_ref, near_ref, half), wo_ref[...]).astype(bf16)

    head_lanes = pl.ds(pl.multiple_of(head * LANE, LANE), LANE)
    keyset = jnp.concatenate([qkv_ref[0, 1], kpos_ref[0]], axis=1)
    keys_turned = qkv_ref[0, 1].T
    values = qkv_ref[0, 2]

    grad_vals[...] = jnp.zeros_like(grad_vals)
    grad_keys[...] = jnp.zeros_like(grad_keys)
    lane = lanes_of((rows, LANE))

    def back(pair, carry):
        val_part = None
        for half in range(2):
            where = pl.ds(pl.multiple_of((2 * pair + half) * rows, rows), rows)
            queries = jnp.concatenate([qkv_ref[0, 0, where, :], qpos_ref[where, :]], axis=1)
            grad_out = dmix[where, head_lanes]
            delta = jnp.sum(
                grad_out.astype(f32) * mix_ref[where, :].astype(f32), axis=1, keepdims=True
            )
            hi, mid, low = split_three(-delta)
            shifted = jnp.where(lane == HEAD, hi, grad_out)
            shifted = jnp.where(lane == HEAD + 1, mid, shifted)
            shifted = jnp.where(lane == HEAD + 2, low, shifted)
            probs = jnp.exp2(dot_nt(keyset, queries) * EXP_SCALE).astype(bf16)
            grad_scores = probs * dot_nt(values, shifted).astype(bf16)
            val_add = dot_nn(probs, grad_out)
            key_add = dot_nn(grad_scores, queries)
            grad_queries[:, where] = dot_nn(keys_turned, grad_scores)
            if val_part is None:
                val_part, key_part = val_add, key_add
            else:
                val_part, key_part = val_part + val_add, key_part + key_add
        grad_vals[...] += val_part
        grad_keys[...] += key_part
        return carry

    lax.fori_loop(0, CHUNKS // 2, back, 0)

    extra = grad_keys[:, LANE:].reshape(grid_side, grid_side, LANE)
    rel_ref[0, 0] = jnp.sum(extra, axis=1)
    rel_ref[0, 1] = jnp.sum(extra, axis=0)
    zeros = jnp.zeros((seq, LANE), f32)
    lane = lanes_of((seq, 256))
    d_query = jnp.concatenate([grad_queries[...].T, zeros], axis=1) * SCALE
    d_keys = pltpu.roll(jnp.concatenate([grad_keys[:, :LANE], zeros], axis=1), HEAD, 1) * SCALE
    d_vals = pltpu.roll(jnp.concatenate([grad_vals[...], zeros], axis=1), 2 * HEAD, 1)
    packed = jnp.where(
        lane < HEAD,
        d_query,
        jnp.where(lane < 2 * HEAD, d_keys, jnp.where(lane < 3 * HEAD, d_vals, 0.0)),
    ).astype(bf16)
    dqkv_ref[:, pl.ds(pl.multiple_of(head * 256, 256), 256)] = packed
    sums_ref[0] = jnp.sum(packed.astype(f32), axis=0, keepdims=True)

    @pl.when(head == heads - 1)
    def _():
        for half in range(2):
            where = pl.ds(half * 2 * rows, 2 * rows)
            put_half(half, dot_nt(dqkv_ref[where, :], w_ref[...]), keep_ref, send_ref)


def attend_back_call(chain, pieces, weights, qkv, qpos, kpos, mixed):
    w_qkv, qkv_start = weights["attend"]
    w_out = weights["out"]
    _, rows, width = pieces[0].shape
    seq = rows * CHUNKS
    heads = kpos.shape[0]
    half = jax.ShapeDtypeStruct((2, rows, width), bf16)
    return chain.call(
        attend_back_body,
        (heads,),
        (*pieces, w_out, qkv, qpos, kpos, mixed, w_qkv),
        [whole_spec((2, rows, width))] * 2
        + [
            whole_spec((width, heads * LANE)),
            pl.BlockSpec((1, 3, seq, LANE), lambda step: (step, 0, 0, 0)),
            whole_spec((seq, LANE)),
            pl.BlockSpec((1, seq, LANE), lambda step: (step, 0, 0)),
            pl.BlockSpec((seq, LANE), lambda step: (0, step)),
            columns_spec(width, heads * 256, qkv_start),
        ],
        [
            whole_spec((seq, heads * 256)),
            pl.BlockSpec((1, 1, 256), lambda step: (step, 0, 0)),
            pl.BlockSpec((1, 2, 32, LANE), lambda step: (step, 0, 0, 0)),
            whole_spec((2, rows, width)),
            whole_spec((2, rows, width)),
        ],
        [
            jax.ShapeDtypeStruct((seq, heads * 256), bf16),
            jax.ShapeDtypeStruct((heads, 1, 256), f32),
            jax.ShapeDtypeStruct((heads, 2, 32, LANE), f32),
            half,
            half,
        ],
        [
            pltpu.VMEM((seq, heads * LANE), bf16),
            pltpu.VMEM((seq, LANE), f32),
            pltpu.VMEM((seq, 256), f32),
            pltpu.VMEM((LANE, seq), f32),
        ],
        BIG,
        1e3,
        0,
        63,
        "attend_bwd",
    )


def column_chunks(hidden):
    return [pl.ds(start, min(512, hidden - start)) for start in range(0, hidden, 512)]


def mlp_body(own_ref, near_ref, up_ref, down_ref, pre_ref, act_ref, keep_ref, send_ref):
    inputs = row_half(own_ref, near_ref, 0)
    total = None
    for columns in column_chunks(up_ref.shape[1]):
        pre = dot_nn(inputs, up_ref[:, columns])
        inner = jnp.tanh(pre * (GELU_A + GELU_A * GELU_B * (pre * pre)))
        act = (0.5 * pre * (1.0 + inner)).astype(bf16)
        pre_ref[:, columns] = pre.astype(bf16)
        act_ref[:, columns] = act
        part = dot_nt(act, down_ref[:, columns])
        total = part if total is None else total + part
    put_half(0, total, keep_ref, send_ref)


def mlp_call(chain, pieces, weights, hidden):
    w_up, up_start = weights["up"]
    w_down, down_start = weights["down"]
    _, rows, width = pieces[0].shape
    seq = rows * CHUNKS
    half = jax.ShapeDtypeStruct((2, rows, width), bf16)
    half_spec = pl.BlockSpec((1, rows, width), lambda step: (step, 0, 0))
    hidden_spec = pl.BlockSpec((2 * rows, hidden), lambda step: (step, 0))
    return chain.call(
        mlp_body,
        (CHUNKS // 2,),
        (*pieces, w_up, w_down),
        [half_spec] * 2
        + [
            columns_spec(width, hidden, up_start),
            columns_spec(width, hidden, down_start),
        ],
        [hidden_spec, hidden_spec, half_spec, half_spec],
        [
            jax.ShapeDtypeStruct((seq, hidden), bf16),
            jax.ShapeDtypeStruct((seq, hidden), bf16),
            half,
            half,
        ],
        [],
        BIG,
        1e3,
        0,
        63,
        "mlp_fwd",
    )


def mlp_back_body(own_ref, near_ref, pre_ref, down_ref, up_ref, dpre_ref, keep_ref, send_ref):
    gradient = row_half(own_ref, near_ref, 0)
    total = None
    for columns in column_chunks(up_ref.shape[1]):
        grad_act = dot_nn(gradient, down_ref[:, columns])
        pre = pre_ref[:, columns].astype(f32)
        square = pre * pre
        inner = jnp.tanh(pre * (GELU_A + GELU_A * GELU_B * square))
        slope = 0.5 * (1.0 + inner) + 0.5 * pre * (1.0 - inner * inner) * (
            GELU_A + 3.0 * GELU_A * GELU_B * square
        )
        grad_pre = (slope * grad_act).astype(bf16)
        dpre_ref[:, columns] = grad_pre
        part = dot_nt(grad_pre, up_ref[:, columns])
        total = part if total is None else total + part
    put_half(0, total, keep_ref, send_ref)


def mlp_back_call(chain, pieces, pre, weights):
    w_up, up_start = weights["up"]
    w_down, down_start = weights["down"]
    _, rows, width = pieces[0].shape
    hidden = pre.shape[1]
    seq = rows * CHUNKS
    half = jax.ShapeDtypeStruct((2, rows, width), bf16)
    half_spec = pl.BlockSpec((1, rows, width), lambda step: (step, 0, 0))
    hidden_spec = pl.BlockSpec((2 * rows, hidden), lambda step: (step, 0))
    return chain.call(
        mlp_back_body,
        (CHUNKS // 2,),
        (*pieces, pre, w_down, w_up),
        [half_spec] * 2
        + [
            hidden_spec,
            columns_spec(width, hidden, down_start),
            columns_spec(width, hidden, up_start),
        ],
        [hidden_spec, half_spec, half_spec],
        [
            jax.ShapeDtypeStruct((seq, hidden), bf16),
            half,
            half,
        ],
        [],
        BIG,
        1e3,
        0,
        63,
        "mlp_bwd",
    )


def add_body(keep_ref, near_ref, out_ref):
    out_ref[...] = (keep_ref[...].astype(f32) + near_ref[...].astype(f32)).astype(bf16)


def add_both_body(keep_ref, near_ref, last_keep_ref, last_near_ref, out_ref, first_ref):
    step = pl.program_id(0)
    last = (last_keep_ref[0].astype(f32) + last_near_ref[0].astype(f32)).astype(bf16)

    @pl.when(step < 2)
    def _():
        add_body(keep_ref, near_ref, out_ref)

    @pl.when(step == 0)
    def _():
        first_ref[0] = last

    @pl.when(step == 2)
    def _():
        out_ref[0] = last


def add_both_call(chain, pair, last_pair):
    _, rows, width = pair[0].shape
    block = (1, rows, width)
    first = pl.BlockSpec(block, lambda step: (jnp.minimum(step, 1), 0, 0))
    last = pl.BlockSpec(block, lambda step: (step // 2, 0, 0))
    return chain.call(
        add_both_body,
        (3,),
        (*pair, *last_pair),
        [first, first, last, last],
        [pl.BlockSpec(block, lambda step: (step, 0, 0)), whole_spec(block)],
        [
            jax.ShapeDtypeStruct((3, rows, width), bf16),
            jax.ShapeDtypeStruct(block, bf16),
        ],
        [],
        SMALL,
        1e3,
        0,
        63,
        "add_both",
    )


def add_steps(chain, keep, near):
    if chain.postpone:
        box = [(keep, near)]
        chain.pending = box
        yield
        return box[0]
    own = add_call(chain, keep, near)
    yield
    return own


def add_call(chain, keep, near):
    _, rows, width = keep.shape
    spec = pl.BlockSpec((1, rows, width), lambda step: (step, 0, 0))
    return chain.call(
        add_body,
        (2,),
        (keep, near),
        [spec, spec],
        [spec],
        [jax.ShapeDtypeStruct(keep.shape, bf16)],
        [],
        SMALL,
        1e3,
        0,
        63,
        "add_near",
    )[0]


def normalize(value):
    average = jnp.mean(value, axis=-1, keepdims=True)
    centred = value - average
    scaling = lax.rsqrt(jnp.mean(centred * centred, axis=-1, keepdims=True) + norm_epsilon)
    return centred * scaling, scaling


def joined_sum(own, far):
    return own[0].astype(f32) + far[0].astype(f32)


def norm_body(*refs, count, extra):
    base, params = refs[0], refs[count]
    value = base[0].astype(f32)
    if count > 1:
        value = value + joined_sum(refs[1], refs[2])
    state_ref, out_ref = refs[count + 1 + extra : count + 3 + extra]
    state_ref[0] = value.astype(bf16)
    normed, _ = normalize(value)
    out_ref[0] = (normed * params[0:1, :] + params[1:2, :]).astype(bf16)
    if extra:
        add_body(refs[count + 1], refs[count + 2], refs[-1])


def chunk_specs(chunks, rows, width):
    block = (1, rows, width)
    return (
        pl.BlockSpec(block, lambda step: (step, 0, 0)),
        pl.BlockSpec(block, lambda step: (chunks - 1 - step, 0, 0)),
    )


def norm_call(chain, base, parts, params):
    chunks, rows, width = base.shape
    spec, turned = chunk_specs(chunks, rows, width)
    pair = chain.take_pair()
    results = chain.call(
        functools.partial(norm_body, count=1 + len(parts), extra=len(pair)),
        (chunks,),
        (base, *parts, params, *pair),
        [spec] + [spec, turned][: len(parts)] + [whole_spec(params.shape)] + [spec] * len(pair),
        [spec, spec] + [spec] * (len(pair) // 2),
        [jax.ShapeDtypeStruct(base.shape, bf16)] * 2
        + [jax.ShapeDtypeStruct(base.shape, bf16)] * (len(pair) // 2),
        [],
        SMALL,
        1e3,
        0,
        63,
        "norm_fwd",
    )
    chain.give_pair(results[2:])
    return results[:2]


def end_body(base_ref, own, far, out_ref):
    out_ref[...] = (base_ref[0].astype(f32) + joined_sum(own, far)).astype(bf16)


def end_call(chain, base, own, far):
    _, rows, width = base.shape
    first = pl.BlockSpec((1, rows, width), lambda step: (0, 0, 0))
    third = pl.BlockSpec((1, rows, width), lambda step: (2, 0, 0))
    return chain.call(
        end_body,
        (1,),
        (base, own, far),
        [first, first, third],
        [whole_spec((rows, width))],
        [jax.ShapeDtypeStruct((rows, width), bf16)],
        [],
        SMALL,
        1e3,
        0,
        63,
        "block_end",
    )[0]


def touch_body():
    pass


def touch_call(chain, far):
    chain.hold(far)
    chain.call(touch_body, (1,), (), [], [], [], [], SMALL, 1e3, 0, 63, "far_ready")


def gate_body(*refs):
    pass


def gate_call(chain, value, other):
    chain.hold(other)
    return chain.call(
        gate_body,
        (1,),
        (value,),
        [pl.BlockSpec(memory_space=pl.ANY)],
        [pl.BlockSpec(memory_space=pl.ANY)],
        [jax.ShapeDtypeStruct(value.shape, value.dtype)],
        [],
        SMALL,
        1e3,
        0,
        63,
        "gate",
        aliases={0: 0},
    )[0]


def norm_back_body(*refs, extra):
    own, far, grad_ref, state_ref, params = refs[:5]
    out_ref, sums_ref = refs[5 + extra : 7 + extra]
    step = pl.program_id(0)
    grad = joined_sum(own, far)
    normed, scaling = normalize(state_ref[0].astype(f32))
    scaled = grad * params[0:1, :]
    inner = scaled - jnp.mean(scaled, axis=-1, keepdims=True)
    inner = inner - normed * jnp.mean(scaled * normed, axis=-1, keepdims=True)
    out_ref[0] = (grad_ref[0].astype(f32) + inner * scaling).astype(out_ref.dtype)
    if extra:
        add_body(refs[5], refs[6], refs[-1])

    @pl.when(step == 0)
    def _():
        sums_ref[...] = jnp.concatenate(
            [
                jnp.sum(grad * normed, axis=0, keepdims=True),
                jnp.sum(grad, axis=0, keepdims=True),
            ],
            axis=0,
        )


def norm_back_call(chain, own, far, gradient, state, params, chunks=2):
    _, rows, width = state.shape
    shape = (chunks, rows, width)
    spec, turned = chunk_specs(chunks, rows, width)
    pair = chain.take_pair() if chunks == 2 else ()
    results = chain.call(
        functools.partial(norm_back_body, extra=len(pair)),
        (chunks,),
        (own, far, gradient, state, params, *pair),
        [spec, turned, spec, spec, whole_spec(params.shape)] + [spec] * len(pair),
        [spec, whole_spec((2, width))] + [spec] * (len(pair) // 2),
        [
            jax.ShapeDtypeStruct(shape, bf16 if chunks == 2 else f32),
            jax.ShapeDtypeStruct((2, width), f32),
        ]
        + [jax.ShapeDtypeStruct(shape, bf16)] * (len(pair) // 2),
        [],
        SMALL,
        1e3,
        0,
        63,
        "norm_bwd",
    )
    chain.give_pair(results[2:])
    return results[:2]


def weight_body(*refs):
    own0, near0, right0, own1, near1, right1 = refs[:6]
    out_ref, total = refs[-2], refs[-1]
    step = pl.program_id(0)
    part = dot_nn(row_half(own0, near0, 0).T, right0[...])
    part = part + dot_nn(row_half(own1, near1, 0).T, right1[...])

    @pl.when(step == 0)
    def _():
        total[...] = part

    @pl.when(step > 0)
    def _():
        out_ref[...] = (total[...] + part).astype(bf16)


def weight_call(chain, lefts, rights, buffer, all_columns, place):
    _, rows, width = lefts[0][0].shape
    columns = rights[0].shape[1]
    left = pl.BlockSpec((1, rows, width), lambda step: (step, 0, 0))
    right = pl.BlockSpec((2 * rows, columns), lambda step: (step, 0))
    inputs = [*lefts[0], rights[0], *lefts[1], rights[1]]
    in_specs = [left, left, right] * 2
    given = None
    if buffer is not None:
        given = {len(inputs): 0}
        inputs.append(buffer)
        in_specs.append(pl.BlockSpec(memory_space=pl.ANY))
    return chain.call(
        weight_body,
        (2,),
        inputs,
        in_specs,
        [pl.BlockSpec((width, columns), lambda step: (0, place))],
        [jax.ShapeDtypeStruct((width, all_columns), bf16)],
        [pltpu.VMEM((width, columns), f32)],
        BIG,
        1e3,
        0,
        63,
        "weight_grad",
        aliases=given,
    )[0]


def swap(value, axis, bit):
    size = lax.axis_size(axis)
    return lax.ppermute(value, axis, [(index, index ^ bit) for index in range(size)])


def total_over(value, axis):
    bit = 1
    while bit < lax.axis_size(axis):
        value = value + swap(value, axis, bit)
        bit *= 2
    return value


def offset_onehot(grid_side):
    places = jnp.arange(grid_side)
    offset = places[:, None] - places[None, :] + grid_side - 1
    return (offset[:, :, None] == jnp.arange(2 * grid_side - 1)[None, None, :]).astype(f32)


def lamb_moments(param, first, second, gradient):
    first_new = beta_first * first + (1.0 - beta_first) * gradient
    second_new = beta_second * second + (1.0 - beta_second) * gradient * gradient
    corrected = first_new / (1.0 - beta_first**STEP)
    update = (
        corrected / (jnp.sqrt(second_new / (1.0 - beta_second**STEP)) + adam_epsilon)
        + decay_rate * param
    )
    return (first_new, second_new, update)


def shards(
    tokens, cotangent, key_mask, group_bucket, group_count, time_table,
    ln_params, ln_first, ln_second, rel_table, rel_first, rel_second,
    qkv_weight, qkv_first, qkv_second, time_weight, time_first, time_second,
    out_weight, out_first, out_second, up_weight, up_first, up_second,
    down_weight, down_first, down_second,
):
    slots, rows, width = tokens.shape
    seq = key_mask.shape[1]
    layers = ln_params.shape[0]
    parts = lax.axis_size("mp")
    groups = lax.axis_size("group")
    heads = rel_table.shape[1] // parts
    buckets = time_table.shape[0]
    grid_side = (rel_table.shape[3] + 1) // 2
    shard_rows = qkv_weight.shape[1]
    local_width = qkv_weight.shape[3]
    place = lax.axis_index("mp")
    group = lax.axis_index("group")
    head_start = place * heads
    order = jnp.arange(CHUNKS) ^ place
    images = range(slots)

    def ready(layer):
        qkv = qkv_weight[layer].astype(bf16).reshape(shard_rows, 3, heads, HEAD)
        qkv = qkv.transpose(0, 2, 1, 3).reshape(shard_rows, heads, 3 * HEAD)
        out = out_weight[layer].astype(bf16).T.reshape(shard_rows, heads, HEAD)
        blocks = jnp.concatenate([qkv, out[:, :, :SPARE]], axis=2).reshape(shard_rows, heads * 256)
        attend = jnp.concatenate(
            [blocks, out[:, :, SPARE:].reshape(shard_rows, heads * (HEAD - SPARE))], axis=1
        )
        up = up_weight[layer].astype(bf16)
        down = down_weight[layer].astype(bf16).T
        return (attend, up, down)

    hidden = up_weight.shape[2]
    fetched = [{} for _ in range(layers)]

    def fetch_together(*wanted):
        parts = [local[layer][kind] for kind, layer in wanted]
        whole = lax.all_gather(jnp.concatenate(parts, axis=1), "group", axis=0, tiled=True)
        start = 0
        for (kind, layer), part in zip(wanted, parts):
            fetched[layer][kind] = (whole, start)
            start += part.shape[1]

    local = [dict(zip(("attend", "up", "down"), ready(layer))) for layer in range(layers)]
    for layer in range(layers):
        fetch_together(("attend", layer))
        fetch_together(("up", layer), ("down", layer))

    table_low = time_table.astype(bf16)
    own_rows = lax.dynamic_slice_in_dim(table_low, group * shard_rows, shard_rows, 1)
    time_part = jnp.einsum(
        "bd,ldf->lbf",
        own_rows,
        time_weight.astype(bf16).reshape(layers, shard_rows, 2 * local_width),
        preferred_element_type=f32,
    )
    early = jnp.concatenate(
        [
            time_part.reshape(layers * buckets, 2 * local_width),
            jnp.full((1, 2 * local_width), group_count[0].astype(f32)),
        ]
    )
    early = total_over(early, "group")
    inverse = 1.0 / early[layers * buckets, 0]
    own_shift = lax.dynamic_index_in_dim(
        early[: layers * buckets].reshape(layers, buckets, 2, heads, HEAD),
        group_bucket[0],
        1,
        keepdims=False,
    )
    zero_shift = jnp.zeros_like(own_shift[:, 0])
    shifts = jnp.concatenate([own_shift[:, 0], zero_shift, own_shift[:, 1]], axis=2)
    shifts = jnp.pad(shifts, ((0, 0), (0, 0), (0, 256 - 3 * HEAD)))[:, :, None, :]

    chunk_side = grid_side // CHUNKS
    row_of = (order[:, None] * chunk_side + jnp.arange(chunk_side)[None]).reshape(grid_side)
    side = jnp.arange(grid_side)
    row_hot = jnp.broadcast_to(
        (row_of[:, None] == side[None])[:, None], (grid_side, grid_side, grid_side)
    )
    col_hot = jnp.broadcast_to(
        (side[:, None] == side[None])[None], (grid_side, grid_side, grid_side)
    )
    hot = jnp.concatenate([row_hot, col_hot], axis=2).reshape(seq, 2 * grid_side)
    qpos = jnp.concatenate([hot, hot], axis=1).astype(bf16)
    onehot = offset_onehot(grid_side)
    own_rel = lax.dynamic_slice_in_dim(rel_table, head_start, heads, 1)
    toeplitz = jnp.einsum("abr,lhpr->lhpba", onehot, own_rel, precision=highest) * ROOT
    row_ext = toeplitz[:, :, 0].reshape(layers, heads, CHUNKS, chunk_side, grid_side)
    row_ext = jnp.take(row_ext, order, axis=2).reshape(layers, heads, grid_side, 1, grid_side)
    full = (layers, heads, grid_side, grid_side, grid_side)
    ext = jnp.concatenate(
        [jnp.broadcast_to(row_ext, full), jnp.broadcast_to(toeplitz[:, :, 1][:, :, None], full)],
        axis=4,
    ).reshape(layers, heads, seq, 2 * grid_side)
    ext_high = lax.reduce_precision(ext, 8, 7)
    kpos = jnp.concatenate([ext_high, ext - ext_high], axis=3).astype(bf16)
    lane = jnp.arange(LANE)
    live = jnp.take(key_mask.reshape(slots, CHUNKS, rows), order, axis=1).reshape(slots, seq)
    aux = jnp.where((lane >= HEAD) & (lane < HEAD + 3), 1.0, 0.0)[None, None]
    aux = jnp.where(
        lane == HEAD + 3, jnp.where(live > 0, 0.0, MASKED)[:, :, None], aux
    ).astype(bf16)

    chain = Chain()
    chain.hold(qpos, kpos, aux)
    slot_live = (jnp.arange(slots) < group_count[0]).astype(f32)
    saved = {}
    work = {}
    ends = {}

    start_rows = jnp.stack([tokens, swap(tokens, "mp", 2)], axis=1)
    start_low = cotangent.astype(f32) * slot_live[:, None, None]
    start_low = jnp.stack([start_low.astype(bf16), swap(start_low.astype(bf16), "mp", 2)], axis=1)

    def far_of(own, last):
        return swap(own[1:], "mp", 2) if last else swap(own, "mp", 2)

    def image_steps(image):
        base, parts = start_rows[image], ()
        for layer in range(layers):
            weights = fetched[layer]
            if layer == 0 and image == images[-1]:
                chain.hold(shifts)
            state, normed = norm_call(chain, base, parts, ln_params[layer, 0:2])
            pieces = (normed, swap(normed, "mp", 1))
            yield
            if layer == 0 and image == 0:
                chain.hold(start_low)
            pieces_one = pieces
            qkv, mixed, keep, send = attend_call(
                chain, pieces, weights, shifts[layer], aux[image], qpos, kpos[layer]
            )
            near = swap(send, "mp", 1)
            yield
            own = yield from add_steps(chain, keep, near)
            parts = (own, far_of(own, False))
            touch_call(chain, parts[1])
            yield
            middle, normed = norm_call(chain, state, parts, ln_params[layer, 2:4])
            pieces = (normed, swap(normed, "mp", 1))
            yield
            pre, act, keep, send = mlp_call(chain, pieces, weights, hidden)
            near = swap(send, "mp", 1)
            saved[layer, image] = (state, pieces_one, qkv, mixed, middle, pieces, pre, act)
            base = middle
            if layer < layers - 1:
                yield
                own = yield from add_steps(chain, keep, near)
                parts = (own, far_of(own, False))
                touch_call(chain, parts[1])
                yield
        yield
        low = start_low[image]
        pieces = (low, swap(low, "mp", 1))
        last_pair = (keep, near)
        for layer in reversed(range(layers)):
            weights = fetched[layer]
            state, pieces_one, qkv, mixed, middle, pieces_two, pre, act = saved[layer, image]
            dpre, keep, send = mlp_back_call(chain, pieces, pre, weights)
            near = swap(send, "mp", 1)
            work["down", layer, image] = (pieces, act)
            work["up", layer, image] = (pieces_two, dpre)
            yield
            if last_pair is not None:
                own, last_own = add_both_call(chain, (keep, near), last_pair)
                far = far_of(own, False)
                ends[image] = (base, last_own, far)
                last_pair = None
                yield
            else:
                own = yield from add_steps(chain, keep, near)
                far = far_of(own, False)
            touch_call(chain, far)
            yield
            low, sums_two = norm_back_call(
                chain, own, far, low, middle, ln_params[layer, 2:3]
            )
            pieces = (low, swap(low, "mp", 1))
            work["out", layer, image] = (pieces, mixed)
            yield
            dqkv, col_sums, rel_part, keep, send = attend_back_call(
                chain, pieces, weights, qkv, qpos, kpos[layer], mixed
            )
            near = swap(send, "mp", 1)
            work["qkv", layer, image] = (pieces_one, dqkv)
            yield
            own = yield from add_steps(chain, keep, near)
            far = far_of(own, layer == 0)
            touch_call(chain, far)
            yield
            low, sums_one = norm_back_call(
                chain, own, far, low, state, ln_params[layer, 0:1], 2 if layer else 1
            )
            pieces = (low, swap(low, "mp", 1)) if layer else None
            work["small", layer, image] = (col_sums, rel_part, sums_one, sums_two)
            yield
        ends["gradient", image] = low[0]

    buffers = {}
    sums = {}
    wholes = {"mlp": 2 * hidden, "attend": heads * (256 + LANE)}
    places = {"up": ("mlp", 0), "down": ("mlp", 1), "qkv": ("attend", 0), "out": ("attend", 2)}

    def unpack_step(layer):
        fetched[layer]["out"] = unpack_call(chain, *fetched[layer]["attend"], heads)

    def end_step(image):
        ends[image] = end_call(chain, *ends[image])

    def weight_step(kind, layer):
        lefts, rights = zip(*(work[kind, layer, image] for image in images))
        target, place = places[kind]
        buffer = buffers.pop((target, layer), None)
        whole = weight_call(chain, lefts, rights, buffer, wholes[target], place)
        if buffer is None:
            buffers[target, layer] = whole
            return
        if (target, layer) == ("attend", 0):
            buffers[target, layer] = whole
        else:
            sums[target, layer] = scatter(whole)

    def scatter(whole):
        return lax.psum_scatter(
            whole.reshape(groups, shard_rows, whole.shape[1]),
            "group",
            scatter_dimension=0,
            tiled=False,
        )

    def last_step():
        whole = gate_call(chain, buffers.pop(("attend", 0)), sums["mlp", 0])
        sums["attend", 0] = scatter(whole)

    runs = [image_steps(image) for image in images]
    for entry in SEQUENCE:
        if entry[0] in "ip":
            chain.postpone = entry[0] == "p"
            next(runs[int(entry[1:])])
        elif entry in ("e0", "e1"):
            end_step(int(entry[1:]))
        elif entry == "last":
            last_step()
        elif entry[:6] == "unpack":
            unpack_step(int(entry[-1]))
        elif entry[:5] == "hold_":
            chain.hold(sums[entry[5:-1], int(entry[-1])])
        else:
            weight_step(entry[:-1], int(entry[-1]))
    for steps in runs:
        next(steps, None)

    block_out = jnp.stack([ends[image] for image in images])
    grads = [ends["gradient", image] for image in images]
    norm_grads = [None] * layers
    rel_grads = [None] * layers
    time_sums = [None] * layers
    for layer in range(layers):

        def both(index):
            return sum(work["small", layer, image][index] for image in images)

        col_sums = both(0)[:, 0, : 3 * HEAD].reshape(heads, 3, HEAD)
        time_sums[layer] = jnp.stack([col_sums[:, 0], col_sums[:, 2]]).reshape(2 * local_width)
        rel_sum = both(1)
        row_sum = rel_sum[:, 0, :, :grid_side].reshape(heads, CHUNKS, chunk_side, grid_side)
        row_sum = jnp.take(row_sum, order, axis=1).reshape(heads, grid_side, grid_side)
        col_sum = rel_sum[:, 1, :, grid_side : 2 * grid_side]
        rel_grads[layer] = jnp.einsum(
            "abr,hpba->hpr", onehot, jnp.stack([row_sum, col_sum], axis=1), precision=highest
        )
        norm_grads[layer] = jnp.concatenate([both(2), both(3)])

    bucket_hot = (jnp.arange(buckets) == group_bucket[0]).astype(f32)
    time_buckets = bucket_hot[None, :, None] * jnp.stack(time_sums)[:, None, :]
    sizes = (time_buckets.size, layers * 4 * width, layers * heads * 2 * (2 * grid_side - 1))
    late = jnp.concatenate(
        [
            time_buckets.reshape(-1),
            jnp.stack(norm_grads).reshape(-1),
            jnp.stack(rel_grads).reshape(-1),
        ]
    )
    late = total_over(jnp.pad(late, (0, -late.size % 1024)).reshape(-1, LANE), "group").reshape(-1)
    time_total = late[: sizes[0]].reshape(layers, buckets, 2 * local_width)
    norm_own = late[sizes[0] : sizes[0] + sizes[1]]
    rel_own = late[sizes[0] + sizes[1] : sum(sizes)].reshape(layers, heads, 2, 2 * grid_side - 1)
    rel_whole = lax.dynamic_update_slice_in_dim(
        jnp.zeros(rel_table.shape, f32), rel_own, head_start, 1
    )
    mixed_sums = jnp.concatenate([norm_own, rel_whole.reshape(-1)])
    mixed_sums = total_over(
        jnp.pad(mixed_sums, (0, -mixed_sums.size % 1024)).reshape(-1, LANE), "mp"
    ).reshape(-1)
    norm_sum = mixed_sums[: sizes[1]].reshape(ln_params.shape)
    rel_sum = mixed_sums[sizes[1] : sizes[1] + rel_table.size].reshape(rel_table.shape)

    tokens_grad = (jnp.stack(grads) * inverse).astype(bf16)
    ln_first_new, ln_second_new, ln_update = lamb_moments(
        ln_params, ln_first, ln_second, norm_sum * inverse
    )
    ln_ratio = jnp.sqrt(jnp.sum(ln_params * ln_params, axis=-1, keepdims=True)) / jnp.sqrt(
        jnp.sum(ln_update * ln_update, axis=-1, keepdims=True)
    )
    ln_new = ln_params - learn_rate * ln_ratio * ln_update
    rel_first_new, rel_second_new, rel_update = lamb_moments(
        rel_table, rel_first, rel_second, rel_sum * inverse
    )
    rel_ratio = jnp.sqrt(jnp.sum(rel_table * rel_table, axis=(1, 2, 3), keepdims=True)) / jnp.sqrt(
        jnp.sum(rel_update * rel_update, axis=(1, 2, 3), keepdims=True)
    )
    rel_new = rel_table - learn_rate * rel_ratio * rel_update

    def unpack(layer):
        attend = sums["attend", layer].astype(f32)
        g_qkv, g_out = attend[:, : heads * 256], attend[:, heads * 256 :]
        g_up, g_down = jnp.split(sums["mlp", layer].astype(f32), 2, axis=1)
        g_qkv = g_qkv.reshape(shard_rows, heads, 256)[:, :, : 3 * HEAD]
        g_qkv = g_qkv.reshape(shard_rows, heads, 3, HEAD).transpose(0, 2, 1, 3)
        g_qkv = g_qkv.reshape(shard_rows, 3, local_width)
        g_time = lax.dot_general(
            own_rows.astype(f32),
            time_total[layer],
            (((0,), (0,)), ((), ())),
            precision=highest,
        ).reshape(shard_rows, 2, local_width)
        g_out = g_out.reshape(shard_rows, heads, LANE)[:, :, :HEAD].reshape(shard_rows, local_width)
        return (g_qkv, g_time, g_out.T, g_up, g_down.T)

    unpacked = [unpack(layer) for layer in range(layers)]
    masters = (qkv_weight, time_weight, out_weight, up_weight, down_weight)
    first_olds = (qkv_first, time_first, out_first, up_first, down_first)
    second_olds = (qkv_second, time_second, out_second, up_second, down_second)
    sectioned = []
    squares = []
    for index in range(5):
        master = masters[index]
        reduced = jnp.stack([unpacked[layer][index] for layer in range(layers)]) * inverse
        first_new, second_new, update = lamb_moments(
            master, first_olds[index], second_olds[index], reduced
        )
        axes = tuple(range(1, master.ndim))
        squares.append(
            jnp.stack([jnp.sum(master * master, axis=axes), jnp.sum(update * update, axis=axes)])
        )
        sectioned.append((first_new, second_new, update))

    def summed(parts):
        totals = jnp.stack(parts, axis=2)
        flat = jnp.pad(totals.reshape(-1), (0, 1024 - totals.size)).reshape(8, LANE)
        flat = total_over(total_over(flat, "group"), "mp")
        return flat.reshape(-1)[: totals.size].reshape(totals.shape)

    totals = jnp.concatenate([summed(squares[:3]), summed(squares[3:])], axis=2)
    weight_norm = jnp.sqrt(totals[0])
    update_norm = jnp.sqrt(totals[1])
    trust_ratio = weight_norm / update_norm
    results = []
    for index in range(5):
        master = masters[index]
        first_new, second_new, update = sectioned[index]
        factor = (learn_rate * trust_ratio[:, index]).reshape((layers,) + (1,) * (master.ndim - 1))
        renewed = master - factor * update
        results.extend([renewed, first_new, second_new, renewed.astype(bf16)])
    matrix_stats = jnp.stack([weight_norm, update_norm, trust_ratio])
    return (
        block_out, tokens_grad, ln_new, ln_first_new, ln_second_new,
        rel_new, rel_first_new, rel_second_new, *results, matrix_stats,
    )


def solution(mesh):
    rows = P("group", "mp", None)
    wide = P(None, "group", None, "mp")
    tall = P(None, "mp", "group")
    flat = P(None, "group", "mp")
    in_specs = (
        (rows, rows, P("group", None), P("group"), P("group"))
        + (P(),) * 7
        + (wide,) * 6
        + (tall,) * 3
        + (flat,) * 3
        + (tall,) * 3
    )
    out_specs = (
        (rows, rows) + (P(),) * 6 + (wide,) * 8 + (tall,) * 4 + (flat,) * 4 + (tall,) * 4 + (P(),)
    )
    return jax.shard_map(shards, mesh=mesh, in_specs=in_specs, out_specs=out_specs, check_vma=False)
```

```python
import functools

import jax
import jax.numpy as jnp
from jax import lax
from jax.experimental import pallas as pl
from jax.experimental.pallas import tpu as pltpu
from jax.sharding import PartitionSpec as P

STEP = 5
highest = lax.Precision.HIGHEST
norm_epsilon = 1e-05
adam_epsilon = 1e-06
beta_first = 0.5
beta_second = 0.5
decay_rate = 0.01
learn_rate = 0.5

HEAD = 72
SPARE = 256 - 3 * HEAD
LANE = 128
CHUNKS = 4
MIB = 1 << 20
MASKED = -1e30
SMALL = 6e7
BIG = 6e6
LOG2E = 1.4426950408889634
GELU_A = 0.7978845608
GELU_B = 0.044715
SCALE = HEAD**-0.5
ROOT = HEAD**0.5
EXP_SCALE = LOG2E * SCALE
SEQUENCE = (
    "i0", "i1", "unpack0", "i0", "i0", "i1", "i0", "p1",
    "i0", "i0", "i1", "p0", "i1", "i1", "i0", "unpack1",
    "p1", "i0", "i0", "i1", "p0", "i1", "i1", "i0",
    "p1", "i0", "i0", "i0", "i1", "i0", "i1", "i1",
    "i1", "up1", "i0", "i1", "i0", "down1", "i0", "i1",
    "p0", "i1", "i1", "out1", "i0", "p1", "i0", "qkv1",
    "i0", "i1", "p0", "i1", "i1", "hold_mlp1", "up0", "i0",
    "p1", "i0", "down0", "i0", "i1", "p0", "i1", "out0",
    "hold_attend1", "i1", "qkv0", "last", "i0", "i1", "i0", "i1",
    "i1", "e0", "e1",
)
bf16 = jnp.bfloat16
f32 = jnp.float32


def dot_nn(left, right):
    return lax.dot_general(left, right, (((1,), (0,)), ((), ())), preferred_element_type=f32)


def dot_nt(left, right):
    return lax.dot_general(left, right, (((1,), (1,)), ((), ())), preferred_element_type=f32)


def split_three(value):
    top = value.astype(bf16)
    rest = value - top.astype(f32)
    middle = rest.astype(bf16)
    last = (rest - middle.astype(f32)).astype(bf16)
    return top, middle, last


def lanes_of(shape):
    return lax.broadcasted_iota(jnp.int32, shape, len(shape) - 1)


def columns_spec(rows, columns, start):
    return pl.BlockSpec((pl.Element(rows), pl.Element(columns)), lambda step: (0, start))


def whole_spec(shape):
    return pl.BlockSpec(shape, lambda step: (0,) * len(shape))


class Chain:
    def __init__(self):
        self.token = None
        self.holds = []
        self.pending = None
        self.postpone = False

    def take_pair(self):
        return () if self.pending is None else self.pending.pop()

    def give_pair(self, result):
        if result:
            self.pending.append(result[0])
            self.pending = None

    def hold(self, *arrays):
        self.holds.extend(arrays)

    def call(self, body, grid, inputs, in_specs, out_specs, out_shape, scratch, flops, moved, exps, limit, name, aliases=None):
        count_in, count_out = len(in_specs), len(out_specs)
        waits = self.holds + ([] if self.token is None else [self.token])
        self.holds = []
        first = len(waits)

        def wrapped(*refs):
            ins = refs[first : first + count_in]
            outs = refs[first + count_in : first + count_in + count_out]
            token_ref = refs[first + count_in + count_out]
            rest = refs[first + count_in + count_out + 1 :]

            @pl.when(pl.program_id(0) == 0)
            def _():
                token_ref[...] = jnp.zeros(token_ref.shape, f32)

            body(*ins, *outs, *rest)

        token_spec = pl.BlockSpec((8, LANE), lambda *steps: (0, 0))
        results = pl.pallas_call(
            wrapped,
            grid=grid,
            in_specs=[pl.BlockSpec(memory_space=pl.ANY)] * first + in_specs,
            out_specs=out_specs + [token_spec],
            out_shape=out_shape + [jax.ShapeDtypeStruct((8, LANE), f32)],
            scratch_shapes=scratch,
            input_output_aliases={first + given: out for given, out in (aliases or {}).items()},
            compiler_params=pltpu.CompilerParams(vmem_limit_bytes=limit * MIB),
            cost_estimate=pl.CostEstimate(
                flops=int(flops), bytes_accessed=int(moved), transcendentals=int(exps)
            ),
            name=name,
        )(*waits, *inputs)
        self.token = results[-1]
        return results[:-1]


def put_half(half, value, keep_ref, send_ref):
    rows = keep_ref.shape[1]
    keep_ref[half] = value[:rows].astype(bf16)
    send_ref[half] = value[rows:].astype(bf16)


def row_half(own_ref, near_ref, half):
    return jnp.concatenate([own_ref[half], near_ref[half]], axis=0)


def unpack_body(packed_ref, out_ref):
    rows = packed_ref.shape[0]
    heads = out_ref.shape[1] // LANE
    lane = lanes_of((rows, LANE))
    rest = packed_ref[:, heads * 256 :].astype(f32)
    for head in range(heads):
        block = packed_ref[:, head * 256 : (head + 1) * 256].astype(f32)
        first = pltpu.roll(block, SPARE, 1)[:, :LANE]
        second = pltpu.roll(rest, (SPARE - head * (HEAD - SPARE)) % LANE, 1)
        value = jnp.where(lane < SPARE, first, jnp.where(lane < HEAD, second, 0.0))
        out_ref[:, head * LANE : (head + 1) * LANE] = value.astype(bf16)


def unpack_call(chain, packed, start, heads):
    width = packed.shape[0]
    rows = 384 if width % 384 == 0 else width
    columns = heads * (256 + HEAD - SPARE)
    return chain.call(
        unpack_body,
        (width // rows,),
        (packed,),
        [pl.BlockSpec((pl.Element(rows), pl.Element(columns)), lambda step: (step * rows, start))],
        [pl.BlockSpec((rows, heads * LANE), lambda step: (step, 0))],
        [jax.ShapeDtypeStruct((width, heads * LANE), bf16)],
        [],
        SMALL,
        1e3,
        0,
        63,
        "unpack_out",
    )[0]


def attend_body(
    own_ref, near_ref, w_ref, shift_ref, aux_ref, qpos_ref, kpos_ref, wo_ref,
    qkv_ref, mix_ref, keep_ref, send_ref,
):
    head = pl.program_id(0)
    heads = pl.num_programs(0)
    rows = own_ref.shape[1]
    seq = rows * CHUNKS
    weight = w_ref[...]

    block_rows = 2 * rows
    for half in range(2):
        where = pl.ds(half * block_rows, block_rows)
        out = dot_nn(row_half(own_ref, near_ref, half), weight) + shift_ref[0]
        lane = lanes_of((block_rows, LANE))
        keys = pltpu.roll(out, 256 - HEAD, 1)[:, :LANE]
        vals = pltpu.roll(out, 256 - 2 * HEAD, 1)[:, :LANE]
        queries = jnp.where(lane < HEAD, out[:, :LANE], jnp.where(lane == HEAD + 3, 1.0, 0.0))
        keys = jnp.where(lane < HEAD, keys, aux_ref[where, :].astype(f32))
        vals = jnp.where(lane < HEAD, vals, jnp.where(lane < HEAD + 3, 1.0, 0.0))
        qkv_ref[0, 0, where, :] = queries.astype(bf16)
        qkv_ref[0, 1, where, :] = keys.astype(bf16)
        qkv_ref[0, 2, where, :] = vals.astype(bf16)

    keyset = jnp.concatenate([qkv_ref[0, 1], kpos_ref[0]], axis=1)
    values = qkv_ref[0, 2]
    mix_lanes = pl.ds(pl.multiple_of(head * LANE, LANE), LANE)

    for start in range(0, seq, rows):
        where = pl.ds(start, rows)
        main = qkv_ref[0, 0, where, :]
        queries = jnp.concatenate([main, qpos_ref[where, :]], axis=1)
        scores = dot_nt(queries, keyset)
        top = jnp.max(scores, axis=1, keepdims=True)
        probs = jnp.exp2((scores - top) * EXP_SCALE).astype(bf16)
        mixed = dot_nn(probs, values)
        total = mixed[:, HEAD : HEAD + 1]
        lane = lanes_of((rows, LANE))
        mix_ref[where, mix_lanes] = jnp.where(lane < HEAD, mixed / total, 0.0).astype(bf16)
        hi, mid, low = split_three(-(top + jnp.log2(total) * (1.0 / EXP_SCALE)))
        main = jnp.where(lane == HEAD, hi, main)
        main = jnp.where(lane == HEAD + 1, mid, main)
        main = jnp.where(lane == HEAD + 2, low, main)
        qkv_ref[0, 0, where, :] = main

    @pl.when(head == heads - 1)
    def _():
        for half in range(2):
            where = pl.ds(half * block_rows, block_rows)
            put_half(half, dot_nt(mix_ref[where, :], wo_ref[...]), keep_ref, send_ref)


def attend_call(chain, pieces, weights, shift, aux, qpos, kpos):
    w_qkv, qkv_start = weights["attend"]
    w_out = weights["out"]
    _, rows, width = pieces[0].shape
    seq = rows * CHUNKS
    heads = kpos.shape[0]
    half = jax.ShapeDtypeStruct((2, rows, width), bf16)
    return chain.call(
        attend_body,
        (heads,),
        (*pieces, w_qkv, shift, aux, qpos, kpos, w_out),
        [whole_spec((2, rows, width))] * 2
        + [
            pl.BlockSpec((width, 256), lambda step: (0, qkv_start // 256 + step)),
            pl.BlockSpec((1, 1, 256), lambda step: (step, 0, 0)),
            whole_spec((seq, LANE)),
            whole_spec((seq, LANE)),
            pl.BlockSpec((1, seq, LANE), lambda step: (step, 0, 0)),
            whole_spec((width, heads * LANE)),
        ],
        [
            pl.BlockSpec((1, 3, seq, LANE), lambda step: (step, 0, 0, 0)),
            whole_spec((seq, heads * LANE)),
            whole_spec((2, rows, width)),
            whole_spec((2, rows, width)),
        ],
        [
            jax.ShapeDtypeStruct((heads, 3, seq, LANE), bf16),
            jax.ShapeDtypeStruct((seq, heads * LANE), bf16),
            half,
            half,
        ],
        [],
        BIG,
        1e3,
        0,
        63,
        "attend_fwd",
    )


def attend_back_body(
    own_ref, near_ref, wo_ref, qkv_ref, qpos_ref, kpos_ref, mix_ref, w_ref,
    dqkv_ref, sums_ref, rel_ref, keep_ref, send_ref,
    dmix, grad_vals, grad_keys, grad_queries,
):
    head = pl.program_id(0)
    heads = pl.num_programs(0)
    rows = own_ref.shape[1]
    seq = rows * CHUNKS
    grid_side = 32

    @pl.when(head == 0)
    def _():
        for half in range(2):
            where = pl.ds(half * 2 * rows, 2 * rows)
            dmix[where, :] = dot_nn(row_half(own_ref, near_ref, half), wo_ref[...]).astype(bf16)

    head_lanes = pl.ds(pl.multiple_of(head * LANE, LANE), LANE)
    keyset = jnp.concatenate([qkv_ref[0, 1], kpos_ref[0]], axis=1)
    keys_turned = qkv_ref[0, 1].T
    values = qkv_ref[0, 2]

    lane = lanes_of((rows, LANE))
    val_part = None
    for start in range(0, seq, rows):
        where = pl.ds(start, rows)
        queries = jnp.concatenate([qkv_ref[0, 0, where, :], qpos_ref[where, :]], axis=1)
        grad_out = dmix[where, head_lanes]
        delta = jnp.sum(
            grad_out.astype(f32) * mix_ref[where, :].astype(f32), axis=1, keepdims=True
        )
        hi, mid, low = split_three(-delta)
        shifted = jnp.where(lane == HEAD, hi, grad_out)
        shifted = jnp.where(lane == HEAD + 1, mid, shifted)
        shifted = jnp.where(lane == HEAD + 2, low, shifted)
        probs = jnp.exp2(dot_nt(keyset, queries) * EXP_SCALE).astype(bf16)
        grad_scores = probs * dot_nt(values, shifted).astype(bf16)
        val_add = dot_nn(probs, grad_out)
        key_add = dot_nn(grad_scores, queries)
        grad_queries[:, where] = dot_nn(keys_turned, grad_scores)
        if val_part is None:
            val_part, key_part = val_add, key_add
        else:
            val_part, key_part = val_part + val_add, key_part + key_add
    grad_vals[...] = val_part
    grad_keys[...] = key_part

    extra = grad_keys[:, LANE:].reshape(grid_side, grid_side, LANE)
    rel_ref[0, 0] = jnp.sum(extra, axis=1)
    rel_ref[0, 1] = jnp.sum(extra, axis=0)
    zeros = jnp.zeros((seq, LANE), f32)
    lane = lanes_of((seq, 256))
    d_query = jnp.concatenate([grad_queries[...].T, zeros], axis=1) * SCALE
    d_keys = pltpu.roll(jnp.concatenate([grad_keys[:, :LANE], zeros], axis=1), HEAD, 1) * SCALE
    d_vals = pltpu.roll(jnp.concatenate([grad_vals[...], zeros], axis=1), 2 * HEAD, 1)
    packed = jnp.where(
        lane < HEAD,
        d_query,
        jnp.where(lane < 2 * HEAD, d_keys, jnp.where(lane < 3 * HEAD, d_vals, 0.0)),
    ).astype(bf16)
    dqkv_ref[:, pl.ds(pl.multiple_of(head * 256, 256), 256)] = packed
    sums_ref[0] = jnp.sum(packed.astype(f32), axis=0, keepdims=True)

    @pl.when(head == heads - 1)
    def _():
        for half in range(2):
            where = pl.ds(half * 2 * rows, 2 * rows)
            put_half(half, dot_nt(dqkv_ref[where, :], w_ref[...]), keep_ref, send_ref)


def attend_back_call(chain, pieces, weights, qkv, qpos, kpos, mixed):
    w_qkv, qkv_start = weights["attend"]
    w_out = weights["out"]
    _, rows, width = pieces[0].shape
    seq = rows * CHUNKS
    heads = kpos.shape[0]
    half = jax.ShapeDtypeStruct((2, rows, width), bf16)
    return chain.call(
        attend_back_body,
        (heads,),
        (*pieces, w_out, qkv, qpos, kpos, mixed, w_qkv),
        [whole_spec((2, rows, width))] * 2
        + [
            whole_spec((width, heads * LANE)),
            pl.BlockSpec((1, 3, seq, LANE), lambda step: (step, 0, 0, 0)),
            whole_spec((seq, LANE)),
            pl.BlockSpec((1, seq, LANE), lambda step: (step, 0, 0)),
            pl.BlockSpec((seq, LANE), lambda step: (0, step)),
            columns_spec(width, heads * 256, qkv_start),
        ],
        [
            whole_spec((seq, heads * 256)),
            pl.BlockSpec((1, 1, 256), lambda step: (step, 0, 0)),
            pl.BlockSpec((1, 2, 32, LANE), lambda step: (step, 0, 0, 0)),
            whole_spec((2, rows, width)),
            whole_spec((2, rows, width)),
        ],
        [
            jax.ShapeDtypeStruct((seq, heads * 256), bf16),
            jax.ShapeDtypeStruct((heads, 1, 256), f32),
            jax.ShapeDtypeStruct((heads, 2, 32, LANE), f32),
            half,
            half,
        ],
        [
            pltpu.VMEM((seq, heads * LANE), bf16),
            pltpu.VMEM((seq, LANE), f32),
            pltpu.VMEM((seq, 256), f32),
            pltpu.VMEM((LANE, seq), f32),
        ],
        BIG,
        1e3,
        0,
        63,
        "attend_bwd",
    )


def column_chunks(hidden):
    first = (hidden // 2 + LANE - 1) // LANE * LANE
    return [pl.ds(0, first), pl.ds(first, hidden - first)]


def mlp_body(own_ref, near_ref, up_ref, down_ref, pre_ref, act_ref, keep_ref, send_ref):
    inputs = row_half(own_ref, near_ref, 0)
    total = None
    for columns in column_chunks(up_ref.shape[1]):
        pre = dot_nn(inputs, up_ref[:, columns])
        inner = jnp.tanh(pre * (GELU_A + GELU_A * GELU_B * (pre * pre)))
        act = (0.5 * pre * (1.0 + inner)).astype(bf16)
        pre_ref[:, columns] = pre.astype(bf16)
        act_ref[:, columns] = act
        part = dot_nt(act, down_ref[:, columns])
        total = part if total is None else total + part
    put_half(0, total, keep_ref, send_ref)


def mlp_call(chain, pieces, weights, hidden):
    w_up, up_start = weights["up"]
    w_down, down_start = weights["down"]
    _, rows, width = pieces[0].shape
    seq = rows * CHUNKS
    half = jax.ShapeDtypeStruct((2, rows, width), bf16)
    half_spec = pl.BlockSpec((1, rows, width), lambda step: (step, 0, 0))
    hidden_spec = pl.BlockSpec((2 * rows, hidden), lambda step: (step, 0))
    return chain.call(
        mlp_body,
        (CHUNKS // 2,),
        (*pieces, w_up, w_down),
        [half_spec] * 2
        + [
            columns_spec(width, hidden, up_start),
            columns_spec(width, hidden, down_start),
        ],
        [hidden_spec, hidden_spec, half_spec, half_spec],
        [
            jax.ShapeDtypeStruct((seq, hidden), bf16),
            jax.ShapeDtypeStruct((seq, hidden), bf16),
            half,
            half,
        ],
        [],
        BIG,
        1e3,
        0,
        63,
        "mlp_fwd",
    )


def mlp_back_body(own_ref, near_ref, pre_ref, down_ref, up_ref, dpre_ref, keep_ref, send_ref):
    gradient = row_half(own_ref, near_ref, 0)
    total = None
    for columns in column_chunks(up_ref.shape[1]):
        grad_act = dot_nn(gradient, down_ref[:, columns])
        pre = pre_ref[:, columns].astype(f32)
        square = pre * pre
        inner = jnp.tanh(pre * (GELU_A + GELU_A * GELU_B * square))
        slope = 0.5 * (1.0 + inner) + 0.5 * pre * (1.0 - inner * inner) * (
            GELU_A + 3.0 * GELU_A * GELU_B * square
        )
        grad_pre = (slope * grad_act).astype(bf16)
        dpre_ref[:, columns] = grad_pre
        part = dot_nt(grad_pre, up_ref[:, columns])
        total = part if total is None else total + part
    put_half(0, total, keep_ref, send_ref)


def mlp_back_call(chain, pieces, pre, weights):
    w_up, up_start = weights["up"]
    w_down, down_start = weights["down"]
    _, rows, width = pieces[0].shape
    hidden = pre.shape[1]
    seq = rows * CHUNKS
    half = jax.ShapeDtypeStruct((2, rows, width), bf16)
    half_spec = pl.BlockSpec((1, rows, width), lambda step: (step, 0, 0))
    hidden_spec = pl.BlockSpec((2 * rows, hidden), lambda step: (step, 0))
    return chain.call(
        mlp_back_body,
        (CHUNKS // 2,),
        (*pieces, pre, w_down, w_up),
        [half_spec] * 2
        + [
            hidden_spec,
            columns_spec(width, hidden, down_start),
            columns_spec(width, hidden, up_start),
        ],
        [hidden_spec, half_spec, half_spec],
        [
            jax.ShapeDtypeStruct((seq, hidden), bf16),
            half,
            half,
        ],
        [],
        BIG,
        1e3,
        0,
        63,
        "mlp_bwd",
    )


def add_body(keep_ref, near_ref, out_ref):
    out_ref[...] = (keep_ref[...].astype(f32) + near_ref[...].astype(f32)).astype(bf16)


def add_both_body(keep_ref, near_ref, last_keep_ref, last_near_ref, out_ref, first_ref):
    step = pl.program_id(0)
    last = (last_keep_ref[0].astype(f32) + last_near_ref[0].astype(f32)).astype(bf16)

    @pl.when(step < 2)
    def _():
        add_body(keep_ref, near_ref, out_ref)

    @pl.when(step == 0)
    def _():
        first_ref[0] = last

    @pl.when(step == 2)
    def _():
        out_ref[0] = last


def add_both_call(chain, pair, last_pair):
    _, rows, width = pair[0].shape
    block = (1, rows, width)
    first = pl.BlockSpec(block, lambda step: (jnp.minimum(step, 1), 0, 0))
    last = pl.BlockSpec(block, lambda step: (step // 2, 0, 0))
    return chain.call(
        add_both_body,
        (3,),
        (*pair, *last_pair),
        [first, first, last, last],
        [pl.BlockSpec(block, lambda step: (step, 0, 0)), whole_spec(block)],
        [
            jax.ShapeDtypeStruct((3, rows, width), bf16),
            jax.ShapeDtypeStruct(block, bf16),
        ],
        [],
        SMALL,
        1e3,
        0,
        63,
        "add_both",
    )


def add_steps(chain, keep, near):
    if chain.postpone:
        box = [(keep, near)]
        chain.pending = box
        yield
        return box[0]
    own = add_call(chain, keep, near)
    yield
    return own


def add_call(chain, keep, near):
    _, rows, width = keep.shape
    spec = pl.BlockSpec((1, rows, width), lambda step: (step, 0, 0))
    return chain.call(
        add_body,
        (2,),
        (keep, near),
        [spec, spec],
        [spec],
        [jax.ShapeDtypeStruct(keep.shape, bf16)],
        [],
        SMALL,
        1e3,
        0,
        63,
        "add_near",
    )[0]


def normalize(value):
    average = jnp.mean(value, axis=-1, keepdims=True)
    centred = value - average
    scaling = lax.rsqrt(jnp.mean(centred * centred, axis=-1, keepdims=True) + norm_epsilon)
    return centred * scaling, scaling


def joined_sum(own, far):
    return own[0].astype(f32) + far[0].astype(f32)


def norm_body(*refs, count, extra):
    base, params = refs[0], refs[count]
    value = base[0].astype(f32)
    if count > 1:
        value = value + joined_sum(refs[1], refs[2])
    state_ref, out_ref = refs[count + 1 + extra : count + 3 + extra]
    state_ref[0] = value.astype(bf16)
    normed, _ = normalize(value)
    out_ref[0] = (normed * params[0:1, :] + params[1:2, :]).astype(bf16)
    if extra:
        add_body(refs[count + 1], refs[count + 2], refs[-1])


def chunk_specs(chunks, rows, width):
    block = (1, rows, width)
    return (
        pl.BlockSpec(block, lambda step: (step, 0, 0)),
        pl.BlockSpec(block, lambda step: (chunks - 1 - step, 0, 0)),
    )


def norm_call(chain, base, parts, params):
    chunks, rows, width = base.shape
    spec, turned = chunk_specs(chunks, rows, width)
    pair = chain.take_pair()
    results = chain.call(
        functools.partial(norm_body, count=1 + len(parts), extra=len(pair)),
        (chunks,),
        (base, *parts, params, *pair),
        [spec] + [spec, turned][: len(parts)] + [whole_spec(params.shape)] + [spec] * len(pair),
        [spec, spec] + [spec] * (len(pair) // 2),
        [jax.ShapeDtypeStruct(base.shape, bf16)] * 2
        + [jax.ShapeDtypeStruct(base.shape, bf16)] * (len(pair) // 2),
        [],
        SMALL,
        1e3,
        0,
        63,
        "norm_fwd",
    )
    chain.give_pair(results[2:])
    return results[:2]


def end_body(base_ref, own, far, out_ref):
    out_ref[...] = (base_ref[0].astype(f32) + joined_sum(own, far)).astype(bf16)


def end_call(chain, base, own, far):
    _, rows, width = base.shape
    first = pl.BlockSpec((1, rows, width), lambda step: (0, 0, 0))
    third = pl.BlockSpec((1, rows, width), lambda step: (2, 0, 0))
    return chain.call(
        end_body,
        (1,),
        (base, own, far),
        [first, first, third],
        [whole_spec((rows, width))],
        [jax.ShapeDtypeStruct((rows, width), bf16)],
        [],
        SMALL,
        1e3,
        0,
        63,
        "block_end",
    )[0]


def touch_body():
    pass


def touch_call(chain, far):
    chain.hold(far)
    chain.call(touch_body, (1,), (), [], [], [], [], SMALL, 1e3, 0, 63, "far_ready")


def gate_body(*refs):
    pass


def gate_call(chain, value, other):
    chain.hold(other)
    return chain.call(
        gate_body,
        (1,),
        (value,),
        [pl.BlockSpec(memory_space=pl.ANY)],
        [pl.BlockSpec(memory_space=pl.ANY)],
        [jax.ShapeDtypeStruct(value.shape, value.dtype)],
        [],
        SMALL,
        1e3,
        0,
        63,
        "gate",
        aliases={0: 0},
    )[0]


def norm_back_body(*refs, extra):
    own, far, grad_ref, state_ref, params = refs[:5]
    out_ref, sums_ref = refs[5 + extra : 7 + extra]
    step = pl.program_id(0)
    grad = joined_sum(own, far)
    normed, scaling = normalize(state_ref[0].astype(f32))
    scaled = grad * params[0:1, :]
    inner = scaled - jnp.mean(scaled, axis=-1, keepdims=True)
    inner = inner - normed * jnp.mean(scaled * normed, axis=-1, keepdims=True)
    out_ref[0] = (grad_ref[0].astype(f32) + inner * scaling).astype(out_ref.dtype)
    if extra:
        add_body(refs[5], refs[6], refs[-1])

    @pl.when(step == 0)
    def _():
        sums_ref[...] = jnp.concatenate(
            [
                jnp.sum(grad * normed, axis=0, keepdims=True),
                jnp.sum(grad, axis=0, keepdims=True),
            ],
            axis=0,
        )


def norm_back_call(chain, own, far, gradient, state, params, chunks=2):
    _, rows, width = state.shape
    shape = (chunks, rows, width)
    spec, turned = chunk_specs(chunks, rows, width)
    pair = chain.take_pair() if chunks == 2 else ()
    results = chain.call(
        functools.partial(norm_back_body, extra=len(pair)),
        (chunks,),
        (own, far, gradient, state, params, *pair),
        [spec, turned, spec, spec, whole_spec(params.shape)] + [spec] * len(pair),
        [spec, whole_spec((2, width))] + [spec] * (len(pair) // 2),
        [
            jax.ShapeDtypeStruct(shape, bf16 if chunks == 2 else f32),
            jax.ShapeDtypeStruct((2, width), f32),
        ]
        + [jax.ShapeDtypeStruct(shape, bf16)] * (len(pair) // 2),
        [],
        SMALL,
        1e3,
        0,
        63,
        "norm_bwd",
    )
    chain.give_pair(results[2:])
    return results[:2]


def weight_body(*refs):
    own0, near0, right0, own1, near1, right1 = refs[:6]
    out_ref, total = refs[-2], refs[-1]
    step = pl.program_id(0)
    left = jnp.concatenate([own0[0], near0[0], own1[0], near1[0]], axis=0)
    part = dot_nn(left.T, jnp.concatenate([right0[...], right1[...]], axis=0))

    @pl.when(step == 0)
    def _():
        total[...] = part

    @pl.when(step > 0)
    def _():
        out_ref[...] = (total[...] + part).astype(bf16)


def weight_call(chain, lefts, rights, buffer, all_columns, place):
    _, rows, width = lefts[0][0].shape
    columns = rights[0].shape[1]
    left = pl.BlockSpec((1, rows, width), lambda step: (step, 0, 0))
    right = pl.BlockSpec((2 * rows, columns), lambda step: (step, 0))
    inputs = [*lefts[0], rights[0], *lefts[1], rights[1]]
    in_specs = [left, left, right] * 2
    given = None
    if buffer is not None:
        given = {len(inputs): 0}
        inputs.append(buffer)
        in_specs.append(pl.BlockSpec(memory_space=pl.ANY))
    return chain.call(
        weight_body,
        (2,),
        inputs,
        in_specs,
        [pl.BlockSpec((width, columns), lambda step: (0, place))],
        [jax.ShapeDtypeStruct((width, all_columns), bf16)],
        [pltpu.VMEM((width, columns), f32)],
        BIG,
        1e3,
        0,
        63,
        "weight_grad",
        aliases=given,
    )[0]


def swap(value, axis, bit):
    size = lax.axis_size(axis)
    return lax.ppermute(value, axis, [(index, index ^ bit) for index in range(size)])


def total_over(value, axis):
    bit = 1
    while bit < lax.axis_size(axis):
        value = value + swap(value, axis, bit)
        bit *= 2
    return value


def offset_onehot(grid_side):
    places = jnp.arange(grid_side)
    offset = places[:, None] - places[None, :] + grid_side - 1
    return (offset[:, :, None] == jnp.arange(2 * grid_side - 1)[None, None, :]).astype(f32)


def lamb_moments(param, first, second, gradient):
    first_new = beta_first * first + (1.0 - beta_first) * gradient
    second_new = beta_second * second + (1.0 - beta_second) * gradient * gradient
    corrected = first_new / (1.0 - beta_first**STEP)
    update = (
        corrected / (jnp.sqrt(second_new / (1.0 - beta_second**STEP)) + adam_epsilon)
        + decay_rate * param
    )
    return (first_new, second_new, update)


def shards(
    tokens, cotangent, key_mask, group_bucket, group_count, time_table,
    ln_params, ln_first, ln_second, rel_table, rel_first, rel_second,
    qkv_weight, qkv_first, qkv_second, time_weight, time_first, time_second,
    out_weight, out_first, out_second, up_weight, up_first, up_second,
    down_weight, down_first, down_second,
):
    slots, rows, width = tokens.shape
    seq = key_mask.shape[1]
    layers = ln_params.shape[0]
    parts = lax.axis_size("mp")
    groups = lax.axis_size("group")
    heads = rel_table.shape[1] // parts
    buckets = time_table.shape[0]
    grid_side = (rel_table.shape[3] + 1) // 2
    shard_rows = qkv_weight.shape[1]
    local_width = qkv_weight.shape[3]
    place = lax.axis_index("mp")
    group = lax.axis_index("group")
    head_start = place * heads
    order = jnp.arange(CHUNKS) ^ place
    images = range(slots)

    def ready(layer):
        qkv = qkv_weight[layer].astype(bf16).reshape(shard_rows, 3, heads, HEAD)
        qkv = qkv.transpose(0, 2, 1, 3).reshape(shard_rows, heads, 3 * HEAD)
        out = out_weight[layer].astype(bf16).T.reshape(shard_rows, heads, HEAD)
        blocks = jnp.concatenate([qkv, out[:, :, :SPARE]], axis=2).reshape(shard_rows, heads * 256)
        attend = jnp.concatenate(
            [blocks, out[:, :, SPARE:].reshape(shard_rows, heads * (HEAD - SPARE))], axis=1
        )
        up = up_weight[layer].astype(bf16)
        down = down_weight[layer].astype(bf16).T
        return (attend, up, down)

    hidden = up_weight.shape[2]
    fetched = [{} for _ in range(layers)]

    def fetch_together(*wanted):
        parts = [local[layer][kind] for kind, layer in wanted]
        whole = lax.all_gather(jnp.concatenate(parts, axis=1), "group", axis=0, tiled=True)
        start = 0
        for (kind, layer), part in zip(wanted, parts):
            fetched[layer][kind] = (whole, start)
            start += part.shape[1]

    local = [dict(zip(("attend", "up", "down"), ready(layer))) for layer in range(layers)]
    for layer in range(layers):
        fetch_together(("attend", layer))
        fetch_together(("up", layer), ("down", layer))

    table_low = time_table.astype(bf16)
    own_rows = lax.dynamic_slice_in_dim(table_low, group * shard_rows, shard_rows, 1)
    time_part = jnp.einsum(
        "bd,ldf->lbf",
        own_rows,
        time_weight.astype(bf16).reshape(layers, shard_rows, 2 * local_width),
        preferred_element_type=f32,
    )
    early = jnp.concatenate(
        [
            time_part.reshape(layers * buckets, 2 * local_width),
            jnp.full((1, 2 * local_width), group_count[0].astype(f32)),
        ]
    )
    early = total_over(early, "group")
    inverse = 1.0 / early[layers * buckets, 0]
    own_shift = lax.dynamic_index_in_dim(
        early[: layers * buckets].reshape(layers, buckets, 2, heads, HEAD),
        group_bucket[0],
        1,
        keepdims=False,
    )
    zero_shift = jnp.zeros_like(own_shift[:, 0])
    shifts = jnp.concatenate([own_shift[:, 0], zero_shift, own_shift[:, 1]], axis=2)
    shifts = jnp.pad(shifts, ((0, 0), (0, 0), (0, 256 - 3 * HEAD)))[:, :, None, :]

    chunk_side = grid_side // CHUNKS
    row_of = (order[:, None] * chunk_side + jnp.arange(chunk_side)[None]).reshape(grid_side)
    side = jnp.arange(grid_side)
    row_hot = jnp.broadcast_to(
        (row_of[:, None] == side[None])[:, None], (grid_side, grid_side, grid_side)
    )
    col_hot = jnp.broadcast_to(
        (side[:, None] == side[None])[None], (grid_side, grid_side, grid_side)
    )
    hot = jnp.concatenate([row_hot, col_hot], axis=2).reshape(seq, 2 * grid_side)
    qpos = jnp.concatenate([hot, hot], axis=1).astype(bf16)
    onehot = offset_onehot(grid_side)
    own_rel = lax.dynamic_slice_in_dim(rel_table, head_start, heads, 1)
    toeplitz = jnp.einsum("abr,lhpr->lhpba", onehot, own_rel, precision=highest) * ROOT
    row_ext = toeplitz[:, :, 0].reshape(layers, heads, CHUNKS, chunk_side, grid_side)
    row_ext = jnp.take(row_ext, order, axis=2).reshape(layers, heads, grid_side, 1, grid_side)
    full = (layers, heads, grid_side, grid_side, grid_side)
    ext = jnp.concatenate(
        [jnp.broadcast_to(row_ext, full), jnp.broadcast_to(toeplitz[:, :, 1][:, :, None], full)],
        axis=4,
    ).reshape(layers, heads, seq, 2 * grid_side)
    ext_high = lax.reduce_precision(ext, 8, 7)
    kpos = jnp.concatenate([ext_high, ext - ext_high], axis=3).astype(bf16)
    lane = jnp.arange(LANE)
    live = jnp.take(key_mask.reshape(slots, CHUNKS, rows), order, axis=1).reshape(slots, seq)
    aux = jnp.where((lane >= HEAD) & (lane < HEAD + 3), 1.0, 0.0)[None, None]
    aux = jnp.where(
        lane == HEAD + 3, jnp.where(live > 0, 0.0, MASKED)[:, :, None], aux
    ).astype(bf16)

    chain = Chain()
    chain.hold(qpos, kpos, aux)
    slot_live = (jnp.arange(slots) < group_count[0]).astype(f32)
    saved = {}
    work = {}
    ends = {}

    start_rows = jnp.stack([tokens, swap(tokens, "mp", 2)], axis=1)
    start_low = cotangent.astype(f32) * slot_live[:, None, None]
    start_low = jnp.stack([start_low.astype(bf16), swap(start_low.astype(bf16), "mp", 2)], axis=1)

    def far_of(own, last):
        return swap(own[1:], "mp", 2) if last else swap(own, "mp", 2)

    def image_steps(image):
        base, parts = start_rows[image], ()
        for layer in range(layers):
            weights = fetched[layer]
            if layer == 0 and image == images[-1]:
                chain.hold(shifts)
            state, normed = norm_call(chain, base, parts, ln_params[layer, 0:2])
            pieces = (normed, swap(normed, "mp", 1))
            yield
            if layer == 0 and image == 0:
                chain.hold(start_low)
            pieces_one = pieces
            qkv, mixed, keep, send = attend_call(
                chain, pieces, weights, shifts[layer], aux[image], qpos, kpos[layer]
            )
            near = swap(send, "mp", 1)
            yield
            own = yield from add_steps(chain, keep, near)
            parts = (own, far_of(own, False))
            touch_call(chain, parts[1])
            yield
            middle, normed = norm_call(chain, state, parts, ln_params[layer, 2:4])
            pieces = (normed, swap(normed, "mp", 1))
            yield
            pre, act, keep, send = mlp_call(chain, pieces, weights, hidden)
            near = swap(send, "mp", 1)
            saved[layer, image] = (state, pieces_one, qkv, mixed, middle, pieces, pre, act)
            base = middle
            if layer < layers - 1:
                yield
                own = yield from add_steps(chain, keep, near)
                parts = (own, far_of(own, False))
                touch_call(chain, parts[1])
                yield
        yield
        low = start_low[image]
        pieces = (low, swap(low, "mp", 1))
        last_pair = (keep, near)
        for layer in reversed(range(layers)):
            weights = fetched[layer]
            state, pieces_one, qkv, mixed, middle, pieces_two, pre, act = saved[layer, image]
            dpre, keep, send = mlp_back_call(chain, pieces, pre, weights)
            near = swap(send, "mp", 1)
            work["down", layer, image] = (pieces, act)
            work["up", layer, image] = (pieces_two, dpre)
            yield
            if last_pair is not None:
                own, last_own = add_both_call(chain, (keep, near), last_pair)
                far = far_of(own, False)
                ends[image] = (base, last_own, far)
                last_pair = None
                yield
            else:
                own = yield from add_steps(chain, keep, near)
                far = far_of(own, False)
            touch_call(chain, far)
            yield
            low, sums_two = norm_back_call(
                chain, own, far, low, middle, ln_params[layer, 2:3]
            )
            pieces = (low, swap(low, "mp", 1))
            work["out", layer, image] = (pieces, mixed)
            yield
            dqkv, col_sums, rel_part, keep, send = attend_back_call(
                chain, pieces, weights, qkv, qpos, kpos[layer], mixed
            )
            near = swap(send, "mp", 1)
            work["qkv", layer, image] = (pieces_one, dqkv)
            yield
            own = yield from add_steps(chain, keep, near)
            far = far_of(own, layer == 0)
            touch_call(chain, far)
            yield
            low, sums_one = norm_back_call(
                chain, own, far, low, state, ln_params[layer, 0:1], 2 if layer else 1
            )
            pieces = (low, swap(low, "mp", 1)) if layer else None
            work["small", layer, image] = (col_sums, rel_part, sums_one, sums_two)
            yield
        ends["gradient", image] = low[0]

    buffers = {}
    sums = {}
    wholes = {"mlp": 2 * hidden, "attend": heads * (256 + LANE)}
    places = {"up": ("mlp", 0), "down": ("mlp", 1), "qkv": ("attend", 0), "out": ("attend", 2)}

    def unpack_step(layer):
        fetched[layer]["out"] = unpack_call(chain, *fetched[layer]["attend"], heads)

    def end_step(image):
        ends[image] = end_call(chain, *ends[image])

    def weight_step(kind, layer):
        lefts, rights = zip(*(work[kind, layer, image] for image in images))
        target, place = places[kind]
        buffer = buffers.pop((target, layer), None)
        whole = weight_call(chain, lefts, rights, buffer, wholes[target], place)
        if buffer is None:
            buffers[target, layer] = whole
            return
        if (target, layer) == ("attend", 0):
            buffers[target, layer] = whole
        else:
            sums[target, layer] = scatter(whole)

    def scatter(whole):
        return lax.psum_scatter(
            whole.reshape(groups, shard_rows, whole.shape[1]),
            "group",
            scatter_dimension=0,
            tiled=False,
        )

    def last_step():
        whole = gate_call(chain, buffers.pop(("attend", 0)), sums["mlp", 0])
        sums["attend", 0] = scatter(whole)

    runs = [image_steps(image) for image in images]
    for entry in SEQUENCE:
        if entry[0] in "ip":
            chain.postpone = entry[0] == "p"
            next(runs[int(entry[1:])])
        elif entry in ("e0", "e1"):
            end_step(int(entry[1:]))
        elif entry == "last":
            last_step()
        elif entry[:6] == "unpack":
            unpack_step(int(entry[-1]))
        elif entry[:5] == "hold_":
            chain.hold(sums[entry[5:-1], int(entry[-1])])
        else:
            weight_step(entry[:-1], int(entry[-1]))
    for steps in runs:
        next(steps, None)

    block_out = jnp.stack([ends[image] for image in images])
    grads = [ends["gradient", image] for image in images]
    norm_grads = [None] * layers
    rel_grads = [None] * layers
    time_sums = [None] * layers
    for layer in range(layers):

        def both(index):
            return sum(work["small", layer, image][index] for image in images)

        col_sums = both(0)[:, 0, : 3 * HEAD].reshape(heads, 3, HEAD)
        time_sums[layer] = jnp.stack([col_sums[:, 0], col_sums[:, 2]]).reshape(2 * local_width)
        rel_sum = both(1)
        row_sum = rel_sum[:, 0, :, :grid_side].reshape(heads, CHUNKS, chunk_side, grid_side)
        row_sum = jnp.take(row_sum, order, axis=1).reshape(heads, grid_side, grid_side)
        col_sum = rel_sum[:, 1, :, grid_side : 2 * grid_side]
        rel_grads[layer] = jnp.einsum(
            "abr,hpba->hpr", onehot, jnp.stack([row_sum, col_sum], axis=1), precision=highest
        )
        norm_grads[layer] = jnp.concatenate([both(2), both(3)])

    bucket_hot = (jnp.arange(buckets) == group_bucket[0]).astype(f32)
    time_buckets = bucket_hot[None, :, None] * jnp.stack(time_sums)[:, None, :]
    sizes = (time_buckets.size, layers * 4 * width, layers * heads * 2 * (2 * grid_side - 1))
    late = jnp.concatenate(
        [
            time_buckets.reshape(-1),
            jnp.stack(norm_grads).reshape(-1),
            jnp.stack(rel_grads).reshape(-1),
        ]
    )
    late = total_over(jnp.pad(late, (0, -late.size % 1024)).reshape(-1, LANE), "group").reshape(-1)
    time_total = late[: sizes[0]].reshape(layers, buckets, 2 * local_width)
    norm_own = late[sizes[0] : sizes[0] + sizes[1]]
    rel_own = late[sizes[0] + sizes[1] : sum(sizes)].reshape(layers, heads, 2, 2 * grid_side - 1)
    rel_whole = lax.dynamic_update_slice_in_dim(
        jnp.zeros(rel_table.shape, f32), rel_own, head_start, 1
    )
    mixed_sums = jnp.concatenate([norm_own, rel_whole.reshape(-1)])
    mixed_sums = total_over(
        jnp.pad(mixed_sums, (0, -mixed_sums.size % 1024)).reshape(-1, LANE), "mp"
    ).reshape(-1)
    norm_sum = mixed_sums[: sizes[1]].reshape(ln_params.shape)
    rel_sum = mixed_sums[sizes[1] : sizes[1] + rel_table.size].reshape(rel_table.shape)

    tokens_grad = (jnp.stack(grads) * inverse).astype(bf16)
    ln_first_new, ln_second_new, ln_update = lamb_moments(
        ln_params, ln_first, ln_second, norm_sum * inverse
    )
    ln_ratio = jnp.sqrt(jnp.sum(ln_params * ln_params, axis=-1, keepdims=True)) / jnp.sqrt(
        jnp.sum(ln_update * ln_update, axis=-1, keepdims=True)
    )
    ln_new = ln_params - learn_rate * ln_ratio * ln_update
    rel_first_new, rel_second_new, rel_update = lamb_moments(
        rel_table, rel_first, rel_second, rel_sum * inverse
    )
    rel_ratio = jnp.sqrt(jnp.sum(rel_table * rel_table, axis=(1, 2, 3), keepdims=True)) / jnp.sqrt(
        jnp.sum(rel_update * rel_update, axis=(1, 2, 3), keepdims=True)
    )
    rel_new = rel_table - learn_rate * rel_ratio * rel_update

    def unpack(layer):
        attend = sums["attend", layer].astype(f32)
        g_qkv, g_out = attend[:, : heads * 256], attend[:, heads * 256 :]
        g_up, g_down = jnp.split(sums["mlp", layer].astype(f32), 2, axis=1)
        g_qkv = g_qkv.reshape(shard_rows, heads, 256)[:, :, : 3 * HEAD]
        g_qkv = g_qkv.reshape(shard_rows, heads, 3, HEAD).transpose(0, 2, 1, 3)
        g_qkv = g_qkv.reshape(shard_rows, 3, local_width)
        g_time = lax.dot_general(
            own_rows.astype(f32),
            time_total[layer],
            (((0,), (0,)), ((), ())),
            precision=highest,
        ).reshape(shard_rows, 2, local_width)
        g_out = g_out.reshape(shard_rows, heads, LANE)[:, :, :HEAD].reshape(shard_rows, local_width)
        return (g_qkv, g_time, g_out.T, g_up, g_down.T)

    unpacked = [unpack(layer) for layer in range(layers)]
    masters = (qkv_weight, time_weight, out_weight, up_weight, down_weight)
    first_olds = (qkv_first, time_first, out_first, up_first, down_first)
    second_olds = (qkv_second, time_second, out_second, up_second, down_second)
    sectioned = []
    squares = []
    for index in range(5):
        master = masters[index]
        reduced = jnp.stack([unpacked[layer][index] for layer in range(layers)]) * inverse
        first_new, second_new, update = lamb_moments(
            master, first_olds[index], second_olds[index], reduced
        )
        axes = tuple(range(1, master.ndim))
        squares.append(
            jnp.stack([jnp.sum(master * master, axis=axes), jnp.sum(update * update, axis=axes)])
        )
        sectioned.append((first_new, second_new, update))

    def summed(parts):
        totals = jnp.stack(parts, axis=2)
        flat = jnp.pad(totals.reshape(-1), (0, 1024 - totals.size)).reshape(8, LANE)
        flat = total_over(total_over(flat, "group"), "mp")
        return flat.reshape(-1)[: totals.size].reshape(totals.shape)

    totals = jnp.concatenate([summed(squares[:3]), summed(squares[3:])], axis=2)
    weight_norm = jnp.sqrt(totals[0])
    update_norm = jnp.sqrt(totals[1])
    trust_ratio = weight_norm / update_norm
    results = []
    for index in range(5):
        master = masters[index]
        first_new, second_new, update = sectioned[index]
        factor = (learn_rate * trust_ratio[:, index]).reshape((layers,) + (1,) * (master.ndim - 1))
        renewed = master - factor * update
        results.extend([renewed, first_new, second_new, renewed.astype(bf16)])
    matrix_stats = jnp.stack([weight_norm, update_norm, trust_ratio])
    return (
        block_out, tokens_grad, ln_new, ln_first_new, ln_second_new,
        rel_new, rel_first_new, rel_second_new, *results, matrix_stats,
    )


def solution(mesh):
    rows = P("group", "mp", None)
    wide = P(None, "group", None, "mp")
    tall = P(None, "mp", "group")
    flat = P(None, "group", "mp")
    in_specs = (
        (rows, rows, P("group", None), P("group"), P("group"))
        + (P(),) * 7
        + (wide,) * 6
        + (tall,) * 3
        + (flat,) * 3
        + (tall,) * 3
    )
    out_specs = (
        (rows, rows) + (P(),) * 6 + (wide,) * 8 + (tall,) * 4 + (flat,) * 4 + (tall,) * 4 + (P(),)
    )
    return jax.shard_map(shards, mesh=mesh, in_specs=in_specs, out_specs=out_specs, check_vma=False)
```

```python
import functools

import jax
import jax.numpy as jnp
from jax import lax
from jax.experimental import pallas as pl
from jax.experimental.pallas import tpu as pltpu
from jax.sharding import PartitionSpec as P

STEP = 5
highest = lax.Precision.HIGHEST
norm_epsilon = 1e-05
adam_epsilon = 1e-06
beta_first = 0.5
beta_second = 0.5
decay_rate = 0.01
learn_rate = 0.5

HEAD = 72
SPARE = 256 - 3 * HEAD
LANE = 128
CHUNKS = 4
MIB = 1 << 20
MASKED = -1e30
SMALL = 6e7
BIG = 6e6
LOG2E = 1.4426950408889634
GELU_A = 0.7978845608
GELU_B = 0.044715
SCALE = HEAD**-0.5
ROOT = HEAD**0.5
EXP_SCALE = LOG2E * SCALE
SEQUENCE = (
    "i0", "i1", "unpack0", "i0", "i0", "i1", "i0", "p1",
    "i0", "i0", "i1", "p0", "i1", "i1", "i0", "unpack1",
    "p1", "i0", "i0", "i1", "p0", "i1", "i1", "i0",
    "p1", "i0", "i0", "i0", "i1", "i0", "i1", "i1",
    "i1", "up1", "i0", "i1", "i0", "down1", "i0", "i1",
    "p0", "i1", "i1", "out1", "i0", "p1", "i0", "qkv1",
    "i0", "i1", "p0", "i1", "i1", "hold_mlp1", "up0", "i0",
    "p1", "i0", "down0", "i0", "i1", "p0", "i1", "out0",
    "hold_attend1", "i1", "qkv0", "last", "i0", "i1", "i0", "i1",
    "i1", "e0", "e1",
)
bf16 = jnp.bfloat16
f32 = jnp.float32


def dot_nn(left, right):
    return lax.dot_general(left, right, (((1,), (0,)), ((), ())), preferred_element_type=f32)


def dot_nt(left, right):
    return lax.dot_general(left, right, (((1,), (1,)), ((), ())), preferred_element_type=f32)


def split_three(value):
    top = value.astype(bf16)
    rest = value - top.astype(f32)
    middle = rest.astype(bf16)
    last = (rest - middle.astype(f32)).astype(bf16)
    return top, middle, last


def lanes_of(shape):
    return lax.broadcasted_iota(jnp.int32, shape, len(shape) - 1)


def columns_spec(rows, columns, start):
    return pl.BlockSpec((pl.Element(rows), pl.Element(columns)), lambda step: (0, start))


def whole_spec(shape):
    return pl.BlockSpec(shape, lambda step: (0,) * len(shape))


class Chain:
    def __init__(self):
        self.token = None
        self.holds = []
        self.pending = None
        self.postpone = False

    def take_pair(self):
        return () if self.pending is None else self.pending.pop()

    def give_pair(self, result):
        if result:
            self.pending.append(result[0])
            self.pending = None

    def hold(self, *arrays):
        self.holds.extend(arrays)

    def call(self, body, grid, inputs, in_specs, out_specs, out_shape, scratch, flops, moved, exps, limit, name, aliases=None):
        count_in, count_out = len(in_specs), len(out_specs)
        waits = self.holds + ([] if self.token is None else [self.token])
        self.holds = []
        first = len(waits)

        def wrapped(*refs):
            ins = refs[first : first + count_in]
            outs = refs[first + count_in : first + count_in + count_out]
            token_ref = refs[first + count_in + count_out]
            rest = refs[first + count_in + count_out + 1 :]

            @pl.when(pl.program_id(0) == 0)
            def _():
                token_ref[...] = jnp.zeros(token_ref.shape, f32)

            body(*ins, *outs, *rest)

        token_spec = pl.BlockSpec((8, LANE), lambda *steps: (0, 0))
        results = pl.pallas_call(
            wrapped,
            grid=grid,
            in_specs=[pl.BlockSpec(memory_space=pl.ANY)] * first + in_specs,
            out_specs=out_specs + [token_spec],
            out_shape=out_shape + [jax.ShapeDtypeStruct((8, LANE), f32)],
            scratch_shapes=scratch,
            input_output_aliases={first + given: out for given, out in (aliases or {}).items()},
            compiler_params=pltpu.CompilerParams(vmem_limit_bytes=limit * MIB),
            cost_estimate=pl.CostEstimate(
                flops=int(flops), bytes_accessed=int(moved), transcendentals=int(exps)
            ),
            name=name,
        )(*waits, *inputs)
        self.token = results[-1]
        return results[:-1]


def put_half(half, value, keep_ref, send_ref):
    rows = keep_ref.shape[1]
    keep_ref[half] = value[:rows].astype(bf16)
    send_ref[half] = value[rows:].astype(bf16)


def row_half(own_ref, near_ref, half):
    return jnp.concatenate([own_ref[half], near_ref[half]], axis=0)


def unpack_body(packed_ref, out_ref):
    rows = packed_ref.shape[0]
    heads = out_ref.shape[1] // LANE
    lane = lanes_of((rows, LANE))
    rest = packed_ref[:, heads * 256 :].astype(f32)
    for head in range(heads):
        block = packed_ref[:, head * 256 : (head + 1) * 256].astype(f32)
        first = pltpu.roll(block, SPARE, 1)[:, :LANE]
        second = pltpu.roll(rest, (SPARE - head * (HEAD - SPARE)) % LANE, 1)
        value = jnp.where(lane < SPARE, first, jnp.where(lane < HEAD, second, 0.0))
        out_ref[:, head * LANE : (head + 1) * LANE] = value.astype(bf16)


def unpack_call(chain, packed, start, heads):
    width = packed.shape[0]
    rows = 384 if width % 384 == 0 else width
    columns = heads * (256 + HEAD - SPARE)
    return chain.call(
        unpack_body,
        (width // rows,),
        (packed,),
        [pl.BlockSpec((pl.Element(rows), pl.Element(columns)), lambda step: (step * rows, start))],
        [pl.BlockSpec((rows, heads * LANE), lambda step: (step, 0))],
        [jax.ShapeDtypeStruct((width, heads * LANE), bf16)],
        [],
        SMALL,
        1e3,
        0,
        63,
        "unpack_out",
    )[0]


def attend_body(
    own_ref, near_ref, w_ref, shift_ref, aux_ref, qpos_ref, kpos_ref, wo_ref,
    qkv_ref, mix_ref, keep_ref, send_ref,
):
    head = pl.program_id(0)
    heads = pl.num_programs(0)
    rows = own_ref.shape[1]
    seq = rows * CHUNKS
    weight = w_ref[...]

    block_rows = 2 * rows
    for half in range(2):
        where = pl.ds(half * block_rows, block_rows)
        out = dot_nn(row_half(own_ref, near_ref, half), weight) + shift_ref[0]
        lane = lanes_of((block_rows, LANE))
        keys = pltpu.roll(out, 256 - HEAD, 1)[:, :LANE]
        vals = pltpu.roll(out, 256 - 2 * HEAD, 1)[:, :LANE]
        queries = jnp.where(lane < HEAD, out[:, :LANE], jnp.where(lane == HEAD + 3, 1.0, 0.0))
        keys = jnp.where(lane < HEAD, keys, aux_ref[where, :].astype(f32))
        vals = jnp.where(lane < HEAD, vals, jnp.where(lane < HEAD + 3, 1.0, 0.0))
        qkv_ref[0, 0, where, :] = queries.astype(bf16)
        qkv_ref[0, 1, where, :] = keys.astype(bf16)
        qkv_ref[0, 2, where, :] = vals.astype(bf16)

    keyset = jnp.concatenate([qkv_ref[0, 1], kpos_ref[0]], axis=1)
    values = qkv_ref[0, 2]
    mix_lanes = pl.ds(pl.multiple_of(head * LANE, LANE), LANE)

    for start in range(0, seq, rows):
        where = pl.ds(start, rows)
        main = qkv_ref[0, 0, where, :]
        queries = jnp.concatenate([main, qpos_ref[where, :]], axis=1)
        scores = dot_nt(queries, keyset)
        top = jnp.max(scores, axis=1, keepdims=True)
        probs = jnp.exp2((scores - top) * EXP_SCALE).astype(bf16)
        mixed = dot_nn(probs, values)
        total = mixed[:, HEAD : HEAD + 1]
        lane = lanes_of((rows, LANE))
        mix_ref[where, mix_lanes] = jnp.where(lane < HEAD, mixed / total, 0.0).astype(bf16)
        hi, mid, low = split_three(-(top + jnp.log2(total) * (1.0 / EXP_SCALE)))
        main = jnp.where(lane == HEAD, hi, main)
        main = jnp.where(lane == HEAD + 1, mid, main)
        main = jnp.where(lane == HEAD + 2, low, main)
        qkv_ref[0, 0, where, :] = main

    @pl.when(head == heads - 1)
    def _():
        for half in range(2):
            where = pl.ds(half * block_rows, block_rows)
            put_half(half, dot_nt(mix_ref[where, :], wo_ref[...]), keep_ref, send_ref)


def attend_call(chain, pieces, weights, shift, aux, qpos, kpos):
    w_qkv, qkv_start = weights["attend"]
    w_out = weights["out"]
    _, rows, width = pieces[0].shape
    seq = rows * CHUNKS
    heads = kpos.shape[0]
    half = jax.ShapeDtypeStruct((2, rows, width), bf16)
    return chain.call(
        attend_body,
        (heads,),
        (*pieces, w_qkv, shift, aux, qpos, kpos, w_out),
        [whole_spec((2, rows, width))] * 2
        + [
            pl.BlockSpec((width, 256), lambda step: (0, qkv_start // 256 + step)),
            pl.BlockSpec((1, 1, 256), lambda step: (step, 0, 0)),
            whole_spec((seq, LANE)),
            whole_spec((seq, LANE)),
            pl.BlockSpec((1, seq, LANE), lambda step: (step, 0, 0)),
            whole_spec((width, heads * LANE)),
        ],
        [
            pl.BlockSpec((1, 3, seq, LANE), lambda step: (step, 0, 0, 0)),
            whole_spec((seq, heads * LANE)),
            whole_spec((2, rows, width)),
            whole_spec((2, rows, width)),
        ],
        [
            jax.ShapeDtypeStruct((heads, 3, seq, LANE), bf16),
            jax.ShapeDtypeStruct((seq, heads * LANE), bf16),
            half,
            half,
        ],
        [],
        BIG,
        1e3,
        0,
        63,
        "attend_fwd",
    )


def attend_back_body(
    own_ref, near_ref, wo_ref, qkv_ref, qpos_ref, kpos_ref, mix_ref, w_ref,
    dqkv_ref, sums_ref, rel_ref, keep_ref, send_ref,
    dmix, grad_vals, grad_keys, grad_queries,
):
    head = pl.program_id(0)
    heads = pl.num_programs(0)
    rows = own_ref.shape[1]
    seq = rows * CHUNKS
    grid_side = 32

    @pl.when(head == 0)
    def _():
        for half in range(2):
            where = pl.ds(half * 2 * rows, 2 * rows)
            dmix[where, :] = dot_nn(row_half(own_ref, near_ref, half), wo_ref[...]).astype(bf16)

    head_lanes = pl.ds(pl.multiple_of(head * LANE, LANE), LANE)
    keyset = jnp.concatenate([qkv_ref[0, 1], kpos_ref[0]], axis=1)
    keys_turned = qkv_ref[0, 1].T
    values = qkv_ref[0, 2]

    lane = lanes_of((rows, LANE))
    val_part = None
    for start in range(0, seq, rows):
        where = pl.ds(start, rows)
        queries = jnp.concatenate([qkv_ref[0, 0, where, :], qpos_ref[where, :]], axis=1)
        grad_out = dmix[where, head_lanes]
        delta = jnp.sum(
            grad_out.astype(f32) * mix_ref[where, :].astype(f32), axis=1, keepdims=True
        )
        hi, mid, low = split_three(-delta)
        shifted = jnp.where(lane == HEAD, hi, grad_out)
        shifted = jnp.where(lane == HEAD + 1, mid, shifted)
        shifted = jnp.where(lane == HEAD + 2, low, shifted)
        probs = jnp.exp2(dot_nt(keyset, queries) * EXP_SCALE).astype(bf16)
        grad_scores = probs * dot_nt(values, shifted).astype(bf16)
        val_add = dot_nn(probs, grad_out)
        key_add = dot_nn(grad_scores, queries)
        grad_queries[:, where] = dot_nn(keys_turned, grad_scores)
        if val_part is None:
            val_part, key_part = val_add, key_add
        else:
            val_part, key_part = val_part + val_add, key_part + key_add
    grad_vals[...] = val_part
    grad_keys[...] = key_part

    extra = grad_keys[:, LANE:].reshape(grid_side, grid_side, LANE)
    rel_ref[0, 0] = jnp.sum(extra, axis=1)
    rel_ref[0, 1] = jnp.sum(extra, axis=0)
    zeros = jnp.zeros((seq, LANE), f32)
    lane = lanes_of((seq, 256))
    d_query = jnp.concatenate([grad_queries[...].T, zeros], axis=1) * SCALE
    d_keys = pltpu.roll(jnp.concatenate([grad_keys[:, :LANE], zeros], axis=1), HEAD, 1) * SCALE
    d_vals = pltpu.roll(jnp.concatenate([grad_vals[...], zeros], axis=1), 2 * HEAD, 1)
    packed = jnp.where(
        lane < HEAD,
        d_query,
        jnp.where(lane < 2 * HEAD, d_keys, jnp.where(lane < 3 * HEAD, d_vals, 0.0)),
    ).astype(bf16)
    dqkv_ref[:, pl.ds(pl.multiple_of(head * 256, 256), 256)] = packed
    sums_ref[0] = jnp.sum(packed.astype(f32), axis=0, keepdims=True)

    @pl.when(head == heads - 1)
    def _():
        for half in range(2):
            where = pl.ds(half * 2 * rows, 2 * rows)
            put_half(half, dot_nt(dqkv_ref[where, :], w_ref[...]), keep_ref, send_ref)


def attend_back_call(chain, pieces, weights, qkv, qpos, kpos, mixed):
    w_qkv, qkv_start = weights["attend"]
    w_out = weights["out"]
    _, rows, width = pieces[0].shape
    seq = rows * CHUNKS
    heads = kpos.shape[0]
    half = jax.ShapeDtypeStruct((2, rows, width), bf16)
    return chain.call(
        attend_back_body,
        (heads,),
        (*pieces, w_out, qkv, qpos, kpos, mixed, w_qkv),
        [whole_spec((2, rows, width))] * 2
        + [
            whole_spec((width, heads * LANE)),
            pl.BlockSpec((1, 3, seq, LANE), lambda step: (step, 0, 0, 0)),
            whole_spec((seq, LANE)),
            pl.BlockSpec((1, seq, LANE), lambda step: (step, 0, 0)),
            pl.BlockSpec((seq, LANE), lambda step: (0, step)),
            columns_spec(width, heads * 256, qkv_start),
        ],
        [
            whole_spec((seq, heads * 256)),
            pl.BlockSpec((1, 1, 256), lambda step: (step, 0, 0)),
            pl.BlockSpec((1, 2, 32, LANE), lambda step: (step, 0, 0, 0)),
            whole_spec((2, rows, width)),
            whole_spec((2, rows, width)),
        ],
        [
            jax.ShapeDtypeStruct((seq, heads * 256), bf16),
            jax.ShapeDtypeStruct((heads, 1, 256), f32),
            jax.ShapeDtypeStruct((heads, 2, 32, LANE), f32),
            half,
            half,
        ],
        [
            pltpu.VMEM((seq, heads * LANE), bf16),
            pltpu.VMEM((seq, LANE), f32),
            pltpu.VMEM((seq, 256), f32),
            pltpu.VMEM((LANE, seq), f32),
        ],
        BIG,
        1e3,
        0,
        63,
        "attend_bwd",
    )


def column_chunks(hidden):
    return [pl.ds(start, min(512, hidden - start)) for start in range(0, hidden, 512)]


def mlp_body(own_ref, near_ref, up_ref, down_ref, pre_ref, act_ref, keep_ref, send_ref):
    inputs = row_half(own_ref, near_ref, 0)
    total = None
    for columns in column_chunks(up_ref.shape[1]):
        pre = dot_nn(inputs, up_ref[:, columns])
        inner = jnp.tanh(pre * (GELU_A + GELU_A * GELU_B * (pre * pre)))
        act = (0.5 * pre * (1.0 + inner)).astype(bf16)
        pre_ref[:, columns] = pre.astype(bf16)
        act_ref[:, columns] = act
        part = dot_nt(act, down_ref[:, columns])
        total = part if total is None else total + part
    put_half(0, total, keep_ref, send_ref)


def mlp_call(chain, pieces, weights, hidden):
    w_up, up_start = weights["up"]
    w_down, down_start = weights["down"]
    _, rows, width = pieces[0].shape
    seq = rows * CHUNKS
    half = jax.ShapeDtypeStruct((2, rows, width), bf16)
    half_spec = pl.BlockSpec((1, rows, width), lambda step: (step, 0, 0))
    hidden_spec = pl.BlockSpec((2 * rows, hidden), lambda step: (step, 0))
    return chain.call(
        mlp_body,
        (CHUNKS // 2,),
        (*pieces, w_up, w_down),
        [half_spec] * 2
        + [
            columns_spec(width, hidden, up_start),
            columns_spec(width, hidden, down_start),
        ],
        [hidden_spec, hidden_spec, half_spec, half_spec],
        [
            jax.ShapeDtypeStruct((seq, hidden), bf16),
            jax.ShapeDtypeStruct((seq, hidden), bf16),
            half,
            half,
        ],
        [],
        BIG,
        1e3,
        0,
        63,
        "mlp_fwd",
    )


def mlp_back_body(own_ref, near_ref, pre_ref, down_ref, up_ref, dpre_ref, keep_ref, send_ref):
    gradient = row_half(own_ref, near_ref, 0)
    total = None
    for columns in column_chunks(up_ref.shape[1]):
        grad_act = dot_nn(gradient, down_ref[:, columns])
        pre = pre_ref[:, columns].astype(f32)
        square = pre * pre
        inner = jnp.tanh(pre * (GELU_A + GELU_A * GELU_B * square))
        slope = 0.5 * (1.0 + inner) + 0.5 * pre * (1.0 - inner * inner) * (
            GELU_A + 3.0 * GELU_A * GELU_B * square
        )
        grad_pre = (slope * grad_act).astype(bf16)
        dpre_ref[:, columns] = grad_pre
        part = dot_nt(grad_pre, up_ref[:, columns])
        total = part if total is None else total + part
    put_half(0, total, keep_ref, send_ref)


def mlp_back_call(chain, pieces, pre, weights):
    w_up, up_start = weights["up"]
    w_down, down_start = weights["down"]
    _, rows, width = pieces[0].shape
    hidden = pre.shape[1]
    seq = rows * CHUNKS
    half = jax.ShapeDtypeStruct((2, rows, width), bf16)
    half_spec = pl.BlockSpec((1, rows, width), lambda step: (step, 0, 0))
    hidden_spec = pl.BlockSpec((2 * rows, hidden), lambda step: (step, 0))
    return chain.call(
        mlp_back_body,
        (CHUNKS // 2,),
        (*pieces, pre, w_down, w_up),
        [half_spec] * 2
        + [
            hidden_spec,
            columns_spec(width, hidden, down_start),
            columns_spec(width, hidden, up_start),
        ],
        [hidden_spec, half_spec, half_spec],
        [
            jax.ShapeDtypeStruct((seq, hidden), bf16),
            half,
            half,
        ],
        [],
        BIG,
        1e3,
        0,
        63,
        "mlp_bwd",
    )


def add_body(keep_ref, near_ref, out_ref):
    out_ref[...] = (keep_ref[...].astype(f32) + near_ref[...].astype(f32)).astype(bf16)


def add_both_body(keep_ref, near_ref, last_keep_ref, last_near_ref, out_ref, first_ref):
    step = pl.program_id(0)
    last = (last_keep_ref[0].astype(f32) + last_near_ref[0].astype(f32)).astype(bf16)

    @pl.when(step < 2)
    def _():
        add_body(keep_ref, near_ref, out_ref)

    @pl.when(step == 0)
    def _():
        first_ref[0] = last

    @pl.when(step == 2)
    def _():
        out_ref[0] = last


def add_both_call(chain, pair, last_pair):
    _, rows, width = pair[0].shape
    block = (1, rows, width)
    first = pl.BlockSpec(block, lambda step: (jnp.minimum(step, 1), 0, 0))
    last = pl.BlockSpec(block, lambda step: (step // 2, 0, 0))
    return chain.call(
        add_both_body,
        (3,),
        (*pair, *last_pair),
        [first, first, last, last],
        [pl.BlockSpec(block, lambda step: (step, 0, 0)), whole_spec(block)],
        [
            jax.ShapeDtypeStruct((3, rows, width), bf16),
            jax.ShapeDtypeStruct(block, bf16),
        ],
        [],
        SMALL,
        1e3,
        0,
        63,
        "add_both",
    )


def add_steps(chain, keep, near):
    if chain.postpone:
        box = [(keep, near)]
        chain.pending = box
        yield
        return box[0]
    own = add_call(chain, keep, near)
    yield
    return own


def add_call(chain, keep, near):
    _, rows, width = keep.shape
    spec = pl.BlockSpec((1, rows, width), lambda step: (step, 0, 0))
    return chain.call(
        add_body,
        (2,),
        (keep, near),
        [spec, spec],
        [spec],
        [jax.ShapeDtypeStruct(keep.shape, bf16)],
        [],
        SMALL,
        1e3,
        0,
        63,
        "add_near",
    )[0]


def normalize(value):
    average = jnp.mean(value, axis=-1, keepdims=True)
    centred = value - average
    scaling = lax.rsqrt(jnp.mean(centred * centred, axis=-1, keepdims=True) + norm_epsilon)
    return centred * scaling, scaling


def joined_sum(own, far):
    return own[0].astype(f32) + far[0].astype(f32)


def norm_body(*refs, count, extra):
    base, params = refs[0], refs[count]
    value = base[0].astype(f32)
    if count > 1:
        value = value + joined_sum(refs[1], refs[2])
    state_ref, out_ref = refs[count + 1 + extra : count + 3 + extra]
    state_ref[0] = value.astype(bf16)
    normed, _ = normalize(value)
    out_ref[0] = (normed * params[0:1, :] + params[1:2, :]).astype(bf16)
    if extra:
        add_body(refs[count + 1], refs[count + 2], refs[-1])


def chunk_specs(chunks, rows, width):
    block = (1, rows, width)
    return (
        pl.BlockSpec(block, lambda step: (step, 0, 0)),
        pl.BlockSpec(block, lambda step: (chunks - 1 - step, 0, 0)),
    )


def norm_call(chain, base, parts, params):
    chunks, rows, width = base.shape
    spec, turned = chunk_specs(chunks, rows, width)
    pair = chain.take_pair()
    results = chain.call(
        functools.partial(norm_body, count=1 + len(parts), extra=len(pair)),
        (chunks,),
        (base, *parts, params, *pair),
        [spec] + [spec, turned][: len(parts)] + [whole_spec(params.shape)] + [spec] * len(pair),
        [spec, spec] + [spec] * (len(pair) // 2),
        [jax.ShapeDtypeStruct(base.shape, bf16)] * 2
        + [jax.ShapeDtypeStruct(base.shape, bf16)] * (len(pair) // 2),
        [],
        SMALL,
        1e3,
        0,
        63,
        "norm_fwd",
    )
    chain.give_pair(results[2:])
    return results[:2]


def end_body(base_ref, own, far, out_ref):
    out_ref[...] = (base_ref[0].astype(f32) + joined_sum(own, far)).astype(bf16)


def end_call(chain, base, own, far):
    _, rows, width = base.shape
    first = pl.BlockSpec((1, rows, width), lambda step: (0, 0, 0))
    third = pl.BlockSpec((1, rows, width), lambda step: (2, 0, 0))
    return chain.call(
        end_body,
        (1,),
        (base, own, far),
        [first, first, third],
        [whole_spec((rows, width))],
        [jax.ShapeDtypeStruct((rows, width), bf16)],
        [],
        SMALL,
        1e3,
        0,
        63,
        "block_end",
    )[0]


def touch_body():
    pass


def touch_call(chain, far):
    chain.hold(far)
    chain.call(touch_body, (1,), (), [], [], [], [], SMALL, 1e3, 0, 63, "far_ready")


def gate_body(*refs):
    pass


def gate_call(chain, value, other):
    chain.hold(other)
    return chain.call(
        gate_body,
        (1,),
        (value,),
        [pl.BlockSpec(memory_space=pl.ANY)],
        [pl.BlockSpec(memory_space=pl.ANY)],
        [jax.ShapeDtypeStruct(value.shape, value.dtype)],
        [],
        SMALL,
        1e3,
        0,
        63,
        "gate",
        aliases={0: 0},
    )[0]


def norm_back_body(*refs, extra):
    own, far, grad_ref, state_ref, params = refs[:5]
    out_ref, sums_ref = refs[5 + extra : 7 + extra]
    step = pl.program_id(0)
    grad = joined_sum(own, far)
    normed, scaling = normalize(state_ref[0].astype(f32))
    scaled = grad * params[0:1, :]
    inner = scaled - jnp.mean(scaled, axis=-1, keepdims=True)
    inner = inner - normed * jnp.mean(scaled * normed, axis=-1, keepdims=True)
    out_ref[0] = (grad_ref[0].astype(f32) + inner * scaling).astype(out_ref.dtype)
    if extra:
        add_body(refs[5], refs[6], refs[-1])

    @pl.when(step == 0)
    def _():
        sums_ref[...] = jnp.concatenate(
            [
                jnp.sum(grad * normed, axis=0, keepdims=True),
                jnp.sum(grad, axis=0, keepdims=True),
            ],
            axis=0,
        )


def norm_back_call(chain, own, far, gradient, state, params, chunks=2):
    _, rows, width = state.shape
    shape = (chunks, rows, width)
    spec, turned = chunk_specs(chunks, rows, width)
    pair = chain.take_pair() if chunks == 2 else ()
    results = chain.call(
        functools.partial(norm_back_body, extra=len(pair)),
        (chunks,),
        (own, far, gradient, state, params, *pair),
        [spec, turned, spec, spec, whole_spec(params.shape)] + [spec] * len(pair),
        [spec, whole_spec((2, width))] + [spec] * (len(pair) // 2),
        [
            jax.ShapeDtypeStruct(shape, bf16 if chunks == 2 else f32),
            jax.ShapeDtypeStruct((2, width), f32),
        ]
        + [jax.ShapeDtypeStruct(shape, bf16)] * (len(pair) // 2),
        [],
        SMALL,
        1e3,
        0,
        63,
        "norm_bwd",
    )
    chain.give_pair(results[2:])
    return results[:2]


def weight_body(*refs, packed):
    own0, near0, right0, own1, near1, right1 = refs[:6]
    out_ref, total = refs[-2], refs[-1]
    step = pl.program_id(0)
    part = dot_nn(row_half(own0, near0, 0).T, right0[...])
    part = part + dot_nn(row_half(own1, near1, 0).T, right1[...])

    @pl.when(step == 0)
    def _():
        total[...] = part

    @pl.when(step > 0)
    def _():
        value = total[...] + part
        if not packed:
            out_ref[...] = value.astype(bf16)
            return
        other_ref = refs[6]
        width, columns = value.shape
        lane, wide = lanes_of((width, LANE)), lanes_of((width, 256))
        rest = jnp.zeros((width, LANE), f32)
        for head in range(columns // 256):
            other = other_ref[:, head * LANE : (head + 1) * LANE].astype(f32)
            shifted = pltpu.roll(jnp.concatenate([other, jnp.zeros_like(other)], axis=1), 3 * HEAD, 1)
            block = value[:, head * 256 : (head + 1) * 256]
            block = jnp.where(wide < 3 * HEAD, block, shifted)
            out_ref[:, head * 256 : (head + 1) * 256] = block.astype(bf16)
            size = HEAD - SPARE
            moved = pltpu.roll(other, (head * size - SPARE) % LANE, 1)
            rest = jnp.where((lane >= head * size) & (lane < (head + 1) * size), moved, rest)
        out_ref[:, columns:] = rest.astype(bf16)


def weight_call(chain, lefts, rights, buffer, all_columns, place, packed=False):
    _, rows, width = lefts[0][0].shape
    columns = rights[0].shape[1]
    left = pl.BlockSpec((1, rows, width), lambda step: (step, 0, 0))
    right = pl.BlockSpec((2 * rows, columns), lambda step: (step, 0))
    inputs = [*lefts[0], rights[0], *lefts[1], rights[1]]
    in_specs = [left, left, right] * 2
    given = None
    out_spec = pl.BlockSpec((width, columns), lambda step: (0, place))
    if packed:
        inputs.append(buffer)
        in_specs.append(whole_spec(buffer.shape))
        out_spec = whole_spec((width, all_columns))
    elif buffer is not None:
        given = {len(inputs): 0}
        inputs.append(buffer)
        in_specs.append(pl.BlockSpec(memory_space=pl.ANY))
    return chain.call(
        functools.partial(weight_body, packed=packed),
        (2,),
        inputs,
        in_specs,
        [out_spec],
        [jax.ShapeDtypeStruct((width, all_columns), bf16)],
        [pltpu.VMEM((width, columns), f32)],
        BIG,
        1e3,
        0,
        63,
        "weight_grad",
        aliases=given,
    )[0]


def swap(value, axis, bit):
    size = lax.axis_size(axis)
    return lax.ppermute(value, axis, [(index, index ^ bit) for index in range(size)])


def total_over(value, axis):
    bit = 1
    while bit < lax.axis_size(axis):
        value = value + swap(value, axis, bit)
        bit *= 2
    return value


def offset_onehot(grid_side):
    places = jnp.arange(grid_side)
    offset = places[:, None] - places[None, :] + grid_side - 1
    return (offset[:, :, None] == jnp.arange(2 * grid_side - 1)[None, None, :]).astype(f32)


def lamb_moments(param, first, second, gradient):
    first_new = beta_first * first + (1.0 - beta_first) * gradient
    second_new = beta_second * second + (1.0 - beta_second) * gradient * gradient
    corrected = first_new / (1.0 - beta_first**STEP)
    update = (
        corrected / (jnp.sqrt(second_new / (1.0 - beta_second**STEP)) + adam_epsilon)
        + decay_rate * param
    )
    return (first_new, second_new, update)


def shards(
    tokens, cotangent, key_mask, group_bucket, group_count, time_table,
    ln_params, ln_first, ln_second, rel_table, rel_first, rel_second,
    qkv_weight, qkv_first, qkv_second, time_weight, time_first, time_second,
    out_weight, out_first, out_second, up_weight, up_first, up_second,
    down_weight, down_first, down_second,
):
    slots, rows, width = tokens.shape
    seq = key_mask.shape[1]
    layers = ln_params.shape[0]
    parts = lax.axis_size("mp")
    groups = lax.axis_size("group")
    heads = rel_table.shape[1] // parts
    buckets = time_table.shape[0]
    grid_side = (rel_table.shape[3] + 1) // 2
    shard_rows = qkv_weight.shape[1]
    local_width = qkv_weight.shape[3]
    place = lax.axis_index("mp")
    group = lax.axis_index("group")
    head_start = place * heads
    order = jnp.arange(CHUNKS) ^ place
    images = range(slots)

    def ready(layer):
        qkv = qkv_weight[layer].astype(bf16).reshape(shard_rows, 3, heads, HEAD)
        qkv = qkv.transpose(0, 2, 1, 3).reshape(shard_rows, heads, 3 * HEAD)
        out = out_weight[layer].astype(bf16).T.reshape(shard_rows, heads, HEAD)
        blocks = jnp.concatenate([qkv, out[:, :, :SPARE]], axis=2).reshape(shard_rows, heads * 256)
        attend = jnp.concatenate(
            [blocks, out[:, :, SPARE:].reshape(shard_rows, heads * (HEAD - SPARE))], axis=1
        )
        up = up_weight[layer].astype(bf16)
        down = down_weight[layer].astype(bf16).T
        return (attend, up, down)

    hidden = up_weight.shape[2]
    fetched = [{} for _ in range(layers)]

    def fetch_together(*wanted):
        parts = [local[layer][kind] for kind, layer in wanted]
        whole = lax.all_gather(jnp.concatenate(parts, axis=1), "group", axis=0, tiled=True)
        start = 0
        for (kind, layer), part in zip(wanted, parts):
            fetched[layer][kind] = (whole, start)
            start += part.shape[1]

    local = [dict(zip(("attend", "up", "down"), ready(layer))) for layer in range(layers)]
    for layer in range(layers):
        fetch_together(("attend", layer))
        fetch_together(("up", layer), ("down", layer))

    table_low = time_table.astype(bf16)
    own_rows = lax.dynamic_slice_in_dim(table_low, group * shard_rows, shard_rows, 1)
    time_part = jnp.einsum(
        "bd,ldf->lbf",
        own_rows,
        time_weight.astype(bf16).reshape(layers, shard_rows, 2 * local_width),
        preferred_element_type=f32,
    )
    early = jnp.concatenate(
        [
            time_part.reshape(layers * buckets, 2 * local_width),
            jnp.full((1, 2 * local_width), group_count[0].astype(f32)),
        ]
    )
    early = total_over(early, "group")
    inverse = 1.0 / early[layers * buckets, 0]
    own_shift = lax.dynamic_index_in_dim(
        early[: layers * buckets].reshape(layers, buckets, 2, heads, HEAD),
        group_bucket[0],
        1,
        keepdims=False,
    )
    zero_shift = jnp.zeros_like(own_shift[:, 0])
    shifts = jnp.concatenate([own_shift[:, 0], zero_shift, own_shift[:, 1]], axis=2)
    shifts = jnp.pad(shifts, ((0, 0), (0, 0), (0, 256 - 3 * HEAD)))[:, :, None, :]

    chunk_side = grid_side // CHUNKS
    row_of = (order[:, None] * chunk_side + jnp.arange(chunk_side)[None]).reshape(grid_side)
    side = jnp.arange(grid_side)
    row_hot = jnp.broadcast_to(
        (row_of[:, None] == side[None])[:, None], (grid_side, grid_side, grid_side)
    )
    col_hot = jnp.broadcast_to(
        (side[:, None] == side[None])[None], (grid_side, grid_side, grid_side)
    )
    hot = jnp.concatenate([row_hot, col_hot], axis=2).reshape(seq, 2 * grid_side)
    qpos = jnp.concatenate([hot, hot], axis=1).astype(bf16)
    onehot = offset_onehot(grid_side)
    own_rel = lax.dynamic_slice_in_dim(rel_table, head_start, heads, 1)
    toeplitz = jnp.einsum("abr,lhpr->lhpba", onehot, own_rel, precision=highest) * ROOT
    row_ext = toeplitz[:, :, 0].reshape(layers, heads, CHUNKS, chunk_side, grid_side)
    row_ext = jnp.take(row_ext, order, axis=2).reshape(layers, heads, grid_side, 1, grid_side)
    full = (layers, heads, grid_side, grid_side, grid_side)
    ext = jnp.concatenate(
        [jnp.broadcast_to(row_ext, full), jnp.broadcast_to(toeplitz[:, :, 1][:, :, None], full)],
        axis=4,
    ).reshape(layers, heads, seq, 2 * grid_side)
    ext_high = lax.reduce_precision(ext, 8, 7)
    kpos = jnp.concatenate([ext_high, ext - ext_high], axis=3).astype(bf16)
    lane = jnp.arange(LANE)
    live = jnp.take(key_mask.reshape(slots, CHUNKS, rows), order, axis=1).reshape(slots, seq)
    aux = jnp.where((lane >= HEAD) & (lane < HEAD + 3), 1.0, 0.0)[None, None]
    aux = jnp.where(
        lane == HEAD + 3, jnp.where(live > 0, 0.0, MASKED)[:, :, None], aux
    ).astype(bf16)

    chain = Chain()
    chain.hold(qpos, kpos, aux)
    slot_live = (jnp.arange(slots) < group_count[0]).astype(f32)
    saved = {}
    work = {}
    ends = {}

    start_rows = jnp.stack([tokens, swap(tokens, "mp", 2)], axis=1)
    start_low = cotangent.astype(f32) * slot_live[:, None, None]
    start_low = jnp.stack([start_low.astype(bf16), swap(start_low.astype(bf16), "mp", 2)], axis=1)

    def far_of(own, last):
        return swap(own[1:], "mp", 2) if last else swap(own, "mp", 2)

    def image_steps(image):
        base, parts = start_rows[image], ()
        for layer in range(layers):
            weights = fetched[layer]
            if layer == 0 and image == images[-1]:
                chain.hold(shifts)
            state, normed = norm_call(chain, base, parts, ln_params[layer, 0:2])
            pieces = (normed, swap(normed, "mp", 1))
            yield
            if layer == 0 and image == 0:
                chain.hold(start_low)
            pieces_one = pieces
            qkv, mixed, keep, send = attend_call(
                chain, pieces, weights, shifts[layer], aux[image], qpos, kpos[layer]
            )
            near = swap(send, "mp", 1)
            yield
            own = yield from add_steps(chain, keep, near)
            parts = (own, far_of(own, False))
            touch_call(chain, parts[1])
            yield
            middle, normed = norm_call(chain, state, parts, ln_params[layer, 2:4])
            pieces = (normed, swap(normed, "mp", 1))
            yield
            pre, act, keep, send = mlp_call(chain, pieces, weights, hidden)
            near = swap(send, "mp", 1)
            saved[layer, image] = (state, pieces_one, qkv, mixed, middle, pieces, pre, act)
            base = middle
            if layer < layers - 1:
                yield
                own = yield from add_steps(chain, keep, near)
                parts = (own, far_of(own, False))
                touch_call(chain, parts[1])
                yield
        yield
        low = start_low[image]
        pieces = (low, swap(low, "mp", 1))
        last_pair = (keep, near)
        for layer in reversed(range(layers)):
            weights = fetched[layer]
            state, pieces_one, qkv, mixed, middle, pieces_two, pre, act = saved[layer, image]
            dpre, keep, send = mlp_back_call(chain, pieces, pre, weights)
            near = swap(send, "mp", 1)
            work["down", layer, image] = (pieces, act)
            work["up", layer, image] = (pieces_two, dpre)
            yield
            if last_pair is not None:
                own, last_own = add_both_call(chain, (keep, near), last_pair)
                far = far_of(own, False)
                ends[image] = (base, last_own, far)
                last_pair = None
                yield
            else:
                own = yield from add_steps(chain, keep, near)
                far = far_of(own, False)
            touch_call(chain, far)
            yield
            low, sums_two = norm_back_call(
                chain, own, far, low, middle, ln_params[layer, 2:3]
            )
            pieces = (low, swap(low, "mp", 1))
            work["out", layer, image] = (pieces, mixed)
            yield
            dqkv, col_sums, rel_part, keep, send = attend_back_call(
                chain, pieces, weights, qkv, qpos, kpos[layer], mixed
            )
            near = swap(send, "mp", 1)
            work["qkv", layer, image] = (pieces_one, dqkv)
            yield
            own = yield from add_steps(chain, keep, near)
            far = far_of(own, layer == 0)
            touch_call(chain, far)
            yield
            low, sums_one = norm_back_call(
                chain, own, far, low, state, ln_params[layer, 0:1], 2 if layer else 1
            )
            pieces = (low, swap(low, "mp", 1)) if layer else None
            work["small", layer, image] = (col_sums, rel_part, sums_one, sums_two)
            yield
        ends["gradient", image] = low[0]

    buffers = {}
    sums = {}
    wholes = {"mlp": 2 * hidden, "attend": heads * (256 + HEAD - SPARE)}
    places = {"up": ("mlp", 0), "down": ("mlp", 1), "qkv": ("attend", 0), "out": ("attend", 0)}

    def unpack_step(layer):
        fetched[layer]["out"] = unpack_call(chain, *fetched[layer]["attend"], heads)

    def end_step(image):
        ends[image] = end_call(chain, *ends[image])

    def weight_step(kind, layer):
        lefts, rights = zip(*(work[kind, layer, image] for image in images))
        target, place = places[kind]
        buffer = buffers.pop((target, layer), None)
        if target == "mlp":
            whole = weight_call(chain, lefts, rights, buffer, wholes[target], place)
        elif buffer is None:
            whole = weight_call(chain, lefts, rights, None, heads * LANE, 0)
        else:
            whole = weight_call(chain, lefts, rights, buffer, wholes[target], 0, True)
        if buffer is None:
            buffers[target, layer] = whole
            return
        if (target, layer) == ("attend", 0):
            buffers[target, layer] = whole
        else:
            sums[target, layer] = scatter(whole)

    def scatter(whole):
        return lax.psum_scatter(
            whole.reshape(groups, shard_rows, whole.shape[1]),
            "group",
            scatter_dimension=0,
            tiled=False,
        )

    def last_step():
        whole = gate_call(chain, buffers.pop(("attend", 0)), sums["mlp", 0])
        sums["attend", 0] = scatter(whole)

    runs = [image_steps(image) for image in images]
    for entry in SEQUENCE:
        if entry[0] in "ip":
            chain.postpone = entry[0] == "p"
            next(runs[int(entry[1:])])
        elif entry in ("e0", "e1"):
            end_step(int(entry[1:]))
        elif entry == "last":
            last_step()
        elif entry[:6] == "unpack":
            unpack_step(int(entry[-1]))
        elif entry[:5] == "hold_":
            chain.hold(sums[entry[5:-1], int(entry[-1])])
        else:
            weight_step(entry[:-1], int(entry[-1]))
    for steps in runs:
        next(steps, None)

    block_out = jnp.stack([ends[image] for image in images])
    grads = [ends["gradient", image] for image in images]
    norm_grads = [None] * layers
    rel_grads = [None] * layers
    time_sums = [None] * layers
    for layer in range(layers):

        def both(index):
            return sum(work["small", layer, image][index] for image in images)

        col_sums = both(0)[:, 0, : 3 * HEAD].reshape(heads, 3, HEAD)
        time_sums[layer] = jnp.stack([col_sums[:, 0], col_sums[:, 2]]).reshape(2 * local_width)
        rel_sum = both(1)
        row_sum = rel_sum[:, 0, :, :grid_side].reshape(heads, CHUNKS, chunk_side, grid_side)
        row_sum = jnp.take(row_sum, order, axis=1).reshape(heads, grid_side, grid_side)
        col_sum = rel_sum[:, 1, :, grid_side : 2 * grid_side]
        rel_grads[layer] = jnp.einsum(
            "abr,hpba->hpr", onehot, jnp.stack([row_sum, col_sum], axis=1), precision=highest
        )
        norm_grads[layer] = jnp.concatenate([both(2), both(3)])

    bucket_hot = (jnp.arange(buckets) == group_bucket[0]).astype(f32)
    time_buckets = bucket_hot[None, :, None] * jnp.stack(time_sums)[:, None, :]
    sizes = (time_buckets.size, layers * 4 * width, layers * heads * 2 * (2 * grid_side - 1))
    late = jnp.concatenate(
        [
            time_buckets.reshape(-1),
            jnp.stack(norm_grads).reshape(-1),
            jnp.stack(rel_grads).reshape(-1),
        ]
    )
    late = total_over(jnp.pad(late, (0, -late.size % 1024)).reshape(-1, LANE), "group").reshape(-1)
    time_total = late[: sizes[0]].reshape(layers, buckets, 2 * local_width)
    norm_own = late[sizes[0] : sizes[0] + sizes[1]]
    rel_own = late[sizes[0] + sizes[1] : sum(sizes)].reshape(layers, heads, 2, 2 * grid_side - 1)
    rel_whole = lax.dynamic_update_slice_in_dim(
        jnp.zeros(rel_table.shape, f32), rel_own, head_start, 1
    )
    mixed_sums = jnp.concatenate([norm_own, rel_whole.reshape(-1)])
    mixed_sums = total_over(
        jnp.pad(mixed_sums, (0, -mixed_sums.size % 1024)).reshape(-1, LANE), "mp"
    ).reshape(-1)
    norm_sum = mixed_sums[: sizes[1]].reshape(ln_params.shape)
    rel_sum = mixed_sums[sizes[1] : sizes[1] + rel_table.size].reshape(rel_table.shape)

    tokens_grad = (jnp.stack(grads) * inverse).astype(bf16)
    ln_first_new, ln_second_new, ln_update = lamb_moments(
        ln_params, ln_first, ln_second, norm_sum * inverse
    )
    ln_ratio = jnp.sqrt(jnp.sum(ln_params * ln_params, axis=-1, keepdims=True)) / jnp.sqrt(
        jnp.sum(ln_update * ln_update, axis=-1, keepdims=True)
    )
    ln_new = ln_params - learn_rate * ln_ratio * ln_update
    rel_first_new, rel_second_new, rel_update = lamb_moments(
        rel_table, rel_first, rel_second, rel_sum * inverse
    )
    rel_ratio = jnp.sqrt(jnp.sum(rel_table * rel_table, axis=(1, 2, 3), keepdims=True)) / jnp.sqrt(
        jnp.sum(rel_update * rel_update, axis=(1, 2, 3), keepdims=True)
    )
    rel_new = rel_table - learn_rate * rel_ratio * rel_update

    def unpack(layer):
        attend = sums["attend", layer].astype(f32)
        blocks = attend[:, : heads * 256].reshape(shard_rows, heads, 256)
        rest = attend[:, heads * 256 :].reshape(shard_rows, heads, HEAD - SPARE)
        g_out = jnp.concatenate([blocks[:, :, 3 * HEAD :], rest], axis=2)
        g_up, g_down = jnp.split(sums["mlp", layer].astype(f32), 2, axis=1)
        g_qkv = blocks[:, :, : 3 * HEAD].reshape(shard_rows, heads, 3, HEAD).transpose(0, 2, 1, 3)
        g_qkv = g_qkv.reshape(shard_rows, 3, local_width)
        g_time = lax.dot_general(
            own_rows.astype(f32),
            time_total[layer],
            (((0,), (0,)), ((), ())),
            precision=highest,
        ).reshape(shard_rows, 2, local_width)
        g_out = g_out.reshape(shard_rows, local_width)
        return (g_qkv, g_time, g_out.T, g_up, g_down.T)

    unpacked = [unpack(layer) for layer in range(layers)]
    masters = (qkv_weight, time_weight, out_weight, up_weight, down_weight)
    first_olds = (qkv_first, time_first, out_first, up_first, down_first)
    second_olds = (qkv_second, time_second, out_second, up_second, down_second)
    sectioned = []
    squares = []
    for index in range(5):
        master = masters[index]
        reduced = jnp.stack([unpacked[layer][index] for layer in range(layers)]) * inverse
        first_new, second_new, update = lamb_moments(
            master, first_olds[index], second_olds[index], reduced
        )
        axes = tuple(range(1, master.ndim))
        squares.append(
            jnp.stack([jnp.sum(master * master, axis=axes), jnp.sum(update * update, axis=axes)])
        )
        sectioned.append((first_new, second_new, update))

    def summed(parts):
        totals = jnp.stack(parts, axis=2)
        flat = jnp.pad(totals.reshape(-1), (0, 1024 - totals.size)).reshape(8, LANE)
        flat = total_over(total_over(flat, "group"), "mp")
        return flat.reshape(-1)[: totals.size].reshape(totals.shape)

    totals = jnp.concatenate([summed(squares[:3]), summed(squares[3:])], axis=2)
    weight_norm = jnp.sqrt(totals[0])
    update_norm = jnp.sqrt(totals[1])
    trust_ratio = weight_norm / update_norm
    results = []
    for index in range(5):
        master = masters[index]
        first_new, second_new, update = sectioned[index]
        factor = (learn_rate * trust_ratio[:, index]).reshape((layers,) + (1,) * (master.ndim - 1))
        renewed = master - factor * update
        results.extend([renewed, first_new, second_new, renewed.astype(bf16)])
    matrix_stats = jnp.stack([weight_norm, update_norm, trust_ratio])
    return (
        block_out, tokens_grad, ln_new, ln_first_new, ln_second_new,
        rel_new, rel_first_new, rel_second_new, *results, matrix_stats,
    )


def solution(mesh):
    rows = P("group", "mp", None)
    wide = P(None, "group", None, "mp")
    tall = P(None, "mp", "group")
    flat = P(None, "group", "mp")
    in_specs = (
        (rows, rows, P("group", None), P("group"), P("group"))
        + (P(),) * 7
        + (wide,) * 6
        + (tall,) * 3
        + (flat,) * 3
        + (tall,) * 3
    )
    out_specs = (
        (rows, rows) + (P(),) * 6 + (wide,) * 8 + (tall,) * 4 + (flat,) * 4 + (tall,) * 4 + (P(),)
    )
    return jax.shard_map(shards, mesh=mesh, in_specs=in_specs, out_specs=out_specs, check_vma=False)
```
